32 devices in a mesh: group: 4 (over y, x), blk: 4 (over z), att: 2 (over core).
Axes of the slice: x: 2, y: 2, z: 4, core: 2. Of those that a mesh axis runs over, the one named last changes fastest.
Arguments:
- tokens: bfloat16 [2048, 4096], P(('group', 'blk')), may hold values from -6 to 6
- routed_experts: int32 [2048, 8], P(('group', 'blk')), may hold values from 0 to 127, all different within a row; in each aligned block of 128 rows (0 to 127, 128 to 255, ...) at most 16 rows name the same one
- act_cotangent: bfloat16 [2048, 8, 768], P(('group', 'blk'), None, 'att'), may hold values from -2.5 to 2.5
- weight_codes: bfloat16 [4096, 4, 2, 768], P('blk', 'group', None, 'att'), may hold values from -0.09375 to 0.09375
- weight_scales: bfloat16 [32, 4, 2, 6], P('blk', 'group', None, 'att'), may hold values from 0.3984375 to 2.5
Outputs:
- gate_up_gradient: bfloat16 [4096, 4, 2, 768], P('blk', 'group', None, 'att')
The draws below stay inside these ranges and needn't reach their ends.
Inputs may be any that keep to these rules, and one draw needn't show every extreme that they name: `routed_experts`: each row names 8 different experts. Among the 128 rows of one device (aligned blocks of 128 rows), no expert is named by more than 16 rows, a bound that some block reaches.
All inputs are finite; a program needn't handle non-finite values.
Results may differ from the reference program's by a relative error of at most 0.023.
Values may be sent and summed in bfloat16 or wider, within the bound.
No kernel may reach another device: no remote copies, remote signals or barrier semaphores. Data moves between devices by JAX's collectives and lax.ppermute only.
A program may use at most 64 MiB of HBM per device.

```python
import math
import jax
import jax.numpy as jnp
import numpy as np
from jax import lax

D = 4096
EXPERTS = 128
TOPK = 8
H = 768
QB = 128
TOK_DEV = 128
CAP = 16
FLIGHT = 4
CYCLE_LEN = 4
TOKENS = 2048


def level_of(key, extent, shards, low, top_value):
    def one(dim, parts):
        draws = jax.random.uniform(jax.random.fold_in(jax.random.fold_in(key, 6), dim), (parts,), jnp.float32, low / len(shards), top_value / len(shards))
        return jnp.repeat(jnp.exp(draws), extent[dim] // parts).reshape((-1,) + (1,) * (len(extent) - dim - 1))

    gain = one(*shards[0])
    for cut in shards[1:]:
        gain = gain * one(*cut)
    return gain


def routed_block(rng, own, number, rows, count, top, limit, skew):
    sequence = jax.random.permutation(rng, count)
    packed, common = load_shares(count, rows * top, limit, skew, True), load_shares(count, rows * top, limit, skew, False)
    places = jnp.arange(count)

    def named(sizes, offset_by):
        used = int((sizes > 0).sum())
        fixed = max(1, used // 4)
        passed = fixed + (places - fixed + offset_by * (used - fixed)) % max(1, count - fixed)
        return jnp.zeros((count,), jnp.int32).at[sequence[jnp.where(places < fixed, places, passed)]].set(jnp.asarray(sizes, jnp.int32))

    sizes = jnp.where(number % 4 == 0, named(packed, number // 4), named(common, number - number // 4 - 1))
    mixed = jax.random.permutation(jax.random.fold_in(own, 3), count)
    source_of, sink = mixed[0:count // 2 * 2:2], mixed[1:count // 2 * 2:2]
    margin = jnp.minimum(sizes[source_of] - 1, limit - sizes[sink]) // 2
    margin = jnp.where((source_of == sequence[0]) | (sink == sequence[0]) | (sizes[sink] == 0), 0, jnp.maximum(margin, 0))
    passed = jax.random.randint(jax.random.fold_in(own, 4), (count // 2,), 0, 1 << 20) % (margin + 1)
    sizes = sizes.at[source_of].add(-passed).at[sink].add(passed)
    members = jnp.searchsorted(jnp.cumsum(sizes), jnp.arange(rows * top), side="right").astype(jnp.int32)
    grid = members.reshape(top, rows).T
    grid = grid[jax.random.permutation(jax.random.fold_in(own, 1), rows)]
    offset_by = jax.random.randint(jax.random.fold_in(own, 2), (rows, 1), 0, top)
    return jnp.take_along_axis(grid, (jnp.arange(top)[None, :] + offset_by) % top, axis=1)


def load_shares(count, total, bound, skew, full):
    loads = [(1 << 20) // math.isqrt(rank ** skew) + 1 for rank in range(1, count + 1)]
    largest = bound if full else min(bound, max(-(-total // count), total * loads[0] // sum(loads)))
    least = 1 if total - largest >= count - 1 else 0
    holding, surplus = [largest] + [least] * (count - 1), total - largest - least * (count - 1)
    while surplus > 0:
        candidates = [i for i in range(1, count) if holding[i] < largest] or [i for i in range(1, count) if holding[i] < bound]
        whole, remaining = sum([loads[i] for i in candidates]), surplus
        for i in candidates:
            extra = min(bound - holding[i], max(1, remaining * loads[i] // whole), surplus)
            holding[i] = holding[i] + extra
            surplus = surplus - extra
    return np.array(holding)


def scatter_about(rng, extent, scale, limit, shards=(), kind=jnp.bfloat16):
    gain = level_of(rng, extent, shards, -0.22, 0.18) if shards else 1.0
    values = jax.random.normal(rng, extent, jnp.float32) * scale * gain
    return jnp.minimum(jnp.maximum(values, -limit), limit).astype(kind)


def setup_inputs(seed: int = 0) -> dict:
    key_of = jax.random.split(jax.random.key(seed), 6)
    tokens = scatter_about(key_of[0], (TOKENS, D), 1.0, 6.0, ((0, 16),))
    routed_experts_keys = jax.random.split(jax.random.fold_in(key_of[1], 1), TOKENS // TOK_DEV)
    routed_experts_turns = jax.random.permutation(jax.random.fold_in(key_of[1], 3), TOKENS // TOK_DEV)
    routed_experts = jax.vmap(lambda own, number: routed_block(jax.random.fold_in(key_of[1], 2), own, number, TOK_DEV, EXPERTS, TOPK, CAP, 2))(routed_experts_keys, routed_experts_turns).reshape((TOKENS, TOPK))
    act_cotangent = scatter_about(key_of[2], (TOKENS, TOPK, H), (2.0 * (EXPERTS / (TOKENS * TOPK)) ** 0.5), 2.5, ((0, 16), (2, 2)))
    weight_codes = scatter_about(key_of[3], (D, FLIGHT, 2, H), D ** -0.5, 0.09375, ((0, 4), (1, 4), (3, 2)))
    weight_scales = jnp.clip(jnp.exp(math.log(2.5) - 1.8364954 * jax.random.uniform(key_of[4], (D // QB, FLIGHT, 2, H // QB), jnp.float32) ** level_of(key_of[4], (D // QB, FLIGHT, 2, H // QB), ((0, 4), (1, 4), (3, 2)), -0.2, 0.2)), 0.3984375, 2.5).astype(jnp.bfloat16)
    return dict(tokens=tokens, routed_experts=routed_experts, act_cotangent=act_cotangent, weight_codes=weight_codes, weight_scales=weight_scales)


def reference(tokens, routed_experts, act_cotangent, weight_codes, weight_scales):
    sources = TOKENS // TOK_DEV
    token_blocks = tokens.astype(jnp.float32).reshape(sources, TOK_DEV, D)
    id_blocks = routed_experts.reshape(sources, TOK_DEV, TOPK)
    cotangent_blocks = act_cotangent.astype(jnp.float32).reshape(sources, TOK_DEV, TOPK, H)
    slot_index = jnp.arange(CAP, dtype=jnp.int32).astype(jnp.float32)

    def one_expert(expert):
        matches = (id_blocks == expert).astype(jnp.float32)
        chosen = jnp.sum(matches, axis=2)
        position = jnp.cumsum(chosen, axis=1) - 1.0
        selector = chosen[:, None, :] * (position[:, None, :] == slot_index[None, :, None]).astype(jnp.float32)
        sent_tokens = jnp.einsum("sct,std->scd", selector, token_blocks)
        pair_cotangent = jnp.einsum("stk,stkh->sth", matches, cotangent_blocks)
        sent_cotangent = jnp.einsum("sct,sth->sch", selector, pair_cotangent)
        code_values = lax.dynamic_index_in_dim(weight_codes, expert, 1, keepdims=False).astype(jnp.float32)
        scale_values = lax.dynamic_index_in_dim(weight_scales, expert, 1, keepdims=False).astype(jnp.float32)
        expanded = jnp.repeat(jnp.repeat(scale_values, QB, axis=0), QB, axis=2)
        weights = lax.optimization_barrier((code_values * expanded).astype(jnp.bfloat16)).astype(jnp.float32)
        gate_up = jnp.einsum("scd,djh->scjh", sent_tokens, weights)
        gate_pre = gate_up[:, :, 0]
        up_pre = gate_up[:, :, 1]
        sigmoid_gate = jax.nn.sigmoid(gate_pre)
        gate_cotangent = sent_cotangent * up_pre * sigmoid_gate * (1.0 + gate_pre * (1.0 - sigmoid_gate))
        up_cotangent = sent_cotangent * gate_pre * sigmoid_gate
        pre_cotangent = jnp.stack([gate_cotangent, up_cotangent], axis=2)
        pre_cotangent = lax.optimization_barrier(pre_cotangent.astype(jnp.bfloat16)).astype(jnp.float32)
        cycle_tokens = sent_tokens.reshape(sources // CYCLE_LEN, CYCLE_LEN, CAP, D)
        cycle_cotangent = pre_cotangent.reshape(sources // CYCLE_LEN, CYCLE_LEN, CAP, 2, H)

        def add_position(running, cycle_place):
            here_tokens = lax.dynamic_index_in_dim(cycle_tokens, cycle_place, 1, keepdims=False)
            here_cotangent = lax.dynamic_index_in_dim(cycle_cotangent, cycle_place, 1, keepdims=False)
            position_term = jnp.einsum("gcd,gcjh->djh", here_tokens, here_cotangent)
            position_term = lax.optimization_barrier(position_term.astype(jnp.bfloat16)).astype(jnp.float32)
            return running + position_term, None

        running, _ = lax.scan(add_position, jnp.zeros((D, 2, H), jnp.float32), jnp.arange(CYCLE_LEN, dtype=jnp.int32))
        return running.astype(jnp.bfloat16)

    gradients = lax.map(one_expert, jnp.arange(FLIGHT, dtype=jnp.int32))
    return jnp.transpose(gradients, (1, 0, 2, 3))
```

```python
import functools

import jax
import jax.numpy as jnp
from jax import lax
from jax.experimental import pallas as pl
from jax.experimental.pallas import tpu as pltpu
from jax.sharding import PartitionSpec as P

CAP = 16
BF16 = jnp.bfloat16
F32 = jnp.float32
VMEM_BYTES = 40 * 1024 * 1024


def call(kernel, out_shape, args, in_specs, out_specs=None, scratch=(), flops=0, nbytes=0):
    vmem = pl.BlockSpec(memory_space=pltpu.VMEM)
    return pl.pallas_call(
        kernel,
        out_shape=out_shape,
        in_specs=in_specs,
        out_specs=jax.tree.map(lambda _: vmem, out_shape) if out_specs is None else out_specs,
        scratch_shapes=scratch,
        compiler_params=pltpu.CompilerParams(vmem_limit_bytes=VMEM_BYTES),
        cost_estimate=pl.CostEstimate(flops=flops, bytes_accessed=nbytes, transcendentals=0),
    )(*args)


VMEM = pl.BlockSpec(memory_space=pltpu.VMEM)
SMEM = pl.BlockSpec(memory_space=pltpu.SMEM)


def dot(a, b, dims=((1,), (0,))):
    return lax.dot_general(a, b, (dims, ((), ())), preferred_element_type=F32)


def iota(shape, dim):
    return lax.broadcasted_iota(jnp.int32, shape, dim)


def pack_kernel(ng, nb, halves, me, tokens, routed, act, *outs):
    top, count = routed.shape
    rows = ng * CAP
    width = tokens.shape[1] // (nb * halves)
    group, block, half = me[0], me[1], me[2]
    ids = routed[...]
    chosen = [jnp.sum((ids == (group ^ s)).astype(F32), axis=0, keepdims=True) for s in range(ng)]
    chosen_rows = jnp.concatenate([jnp.broadcast_to(c, (CAP, count)) for c in chosen], axis=0)
    upto = (iota((count, count), 0) <= iota((count, count), 1)).astype(F32).astype(BF16)
    place = dot(chosen_rows.astype(BF16), upto)
    slot = (iota((rows, count), 0) % CAP + 1).astype(F32)
    selector = jnp.where(place == slot, chosen_rows, 0.0).astype(BF16)
    spread = (iota((count, count * top), 1) // top == iota((count, count * top), 0)).astype(F32).astype(BF16)
    ids_wide = dot(ids.astype(F32).astype(BF16), spread)
    own_slot = iota((top, count * top), 1) % top == iota((top, count * top), 0)
    ids_flat = jnp.sum(jnp.where(own_slot, ids_wide, 0.0), axis=0, keepdims=True)
    expert = (group ^ (iota((rows, 1), 0) // CAP)).astype(F32)
    pair = jnp.where(ids_flat == expert, dot(selector, spread), 0.0).astype(BF16)
    hidden = act.shape[2]
    cot = dot(pair, act[...].reshape(count * top, hidden)).astype(BF16)
    for p in range(nb):
        start = pl.multiple_of(((block ^ p) * halves + half) * width, width)
        part = dot(selector, tokens[:, pl.ds(start, width)]).astype(BF16)
        for s in range(ng):
            outs[s][:, p * width : (p + 1) * width] = part[s * CAP : (s + 1) * CAP]
    for s in range(ng):
        outs[s][:, nb * width :] = cot[s * CAP : (s + 1) * CAP]


def regroup_kernel(ng, nb, width, *refs):
    pieces, outs = refs[:ng], refs[ng:]
    for s in range(ng):
        for p in range(nb):
            outs[p][s * CAP : (s + 1) * CAP, :] = pieces[s][:, p * width : (p + 1) * width]
        outs[nb][s * CAP : (s + 1) * CAP, :] = pieces[s][:, nb * width :]


def weights_kernel(halves, me, scales, codes, out):
    depth, _, hidden = codes.shape
    blocks, _, cols = scales.shape
    qrows, qcols = depth // blocks, hidden // cols
    half = me[2]
    per_half = blocks // halves
    pick = [
        (iota((qrows, 2 * qrows), 1) == 2 * iota((qrows, 2 * qrows), 0) + j).astype(F32).astype(BF16)
        for j in range(2)
    ]
    for q in range(blocks):
        source = (q + half * per_half) % blocks if halves > 1 else q
        rows = codes[pl.ds(pl.multiple_of(source * qrows, qrows), qrows)].reshape(2 * qrows, hidden)
        for j in range(2):
            values = dot(pick[j], rows)
            for c in range(cols):
                at = j * hidden + c * qcols
                out[q * qrows : (q + 1) * qrows, at : at + qcols] = (
                    values[:, c * qcols : (c + 1) * qcols] * scales[source, j, c]
                ).astype(BF16)


def gate_up_kernel(nb, halves, *refs):
    pieces, weights, outs = refs[: nb * halves], refs[nb * halves], refs[nb * halves + 1 :]
    rows, width = pieces[0].shape
    for p in range(nb):
        total = dot(pieces[p][...], weights[:width])
        for h in range(1, halves):
            total += dot(pieces[h * nb + p][...], weights[h * width : (h + 1) * width])
        outs[p][...] = total.astype(outs[p].dtype)


def swiglu_kernel(nb, *refs):
    parts, cot, out = refs[:nb], refs[nb], refs[nb + 1]
    hidden = cot.shape[1]
    total = parts[0][...]
    for p in range(1, nb):
        total += parts[p][...].astype(F32)
    gate, up = total[:, :hidden], total[:, hidden:]
    c = cot[...].astype(F32)
    s = jax.nn.sigmoid(gate)
    out[:, :hidden] = (c * up * s * (1.0 + gate * (1.0 - s))).astype(BF16)
    out[:, hidden:] = (c * gate * s).astype(BF16)


def spread_kernel(nb, halves, me, *refs):
    pieces, out = refs[: nb * halves], refs[nb * halves]
    rows, width = pieces[0].shape
    step = min(128, width)
    half = me[2]
    put = [
        (iota((2 * step, step), 0) == 2 * iota((2 * step, step), 1) + j).astype(F32).astype(BF16)
        for j in range(2)
    ]
    for h in range(halves):
        for p in range(nb):
            for k in range(width // step):
                block = pieces[h * nb + p][:, k * step : (k + 1) * step]
                start = ((half ^ h) * width + k * step) * 2
                for j in range(2):
                    at = (j * nb + p) * rows
                    out[pl.ds(pl.multiple_of(start, 2 * step), 2 * step), at : at + rows] = dot(
                        put[j], block, ((1,), (1,))
                    ).astype(BF16)


def gradient_kernel(nb, *refs):
    parts, spread, out, stacked = refs[:nb], refs[nb], refs[nb + 1], refs[nb + 2]
    rows = parts[0].shape[0]
    hidden = out.shape[2]
    for j in range(2):
        for p in range(nb):
            at = (j * nb + p) * rows
            stacked[at : at + rows, :] = parts[p][:, j * hidden : (j + 1) * hidden]
    step = min(256, spread.shape[0])
    for k in range(spread.shape[0] // step):
        values = dot(spread[k * step : (k + 1) * step, :], stacked[...])
        out[k * step // 2 : (k + 1) * step // 2] = values.reshape(step // 2, 2, hidden).astype(BF16)


def swap(x, axis, size, s):
    return lax.ppermute(x, axis, [(i, i ^ s) for i in range(size)])


def local(tokens, routed_experts, act_cotangent, weight_codes, weight_scales):
    ng, nb, na = lax.axis_size("group"), lax.axis_size("blk"), lax.axis_size("att")
    depth, _, _, hidden = weight_codes.shape
    halves = 2 if na == 2 and depth % 256 == 0 else 1
    width = depth // halves
    rows = ng * CAP
    me = jnp.stack(
        [lax.axis_index("group"), lax.axis_index("blk"), lax.axis_index("att") if halves == 2 else 0]
    ).astype(jnp.int32)
    sds = jax.ShapeDtypeStruct
    sent = call(
        functools.partial(pack_kernel, ng, nb, halves),
        [sds((CAP, nb * width + hidden), BF16)] * ng,
        (me, tokens, routed_experts.T, act_cotangent),
        [SMEM, VMEM, VMEM, VMEM],
        nbytes=2 << 20,
    )
    pieces = [sent[0]] + [swap(sent[s], "group", ng, s) for s in range(1, ng)]
    *columns, cot = call(
        functools.partial(regroup_kernel, ng, nb, width),
        [sds((rows, width), BF16)] * nb + [sds((rows, hidden), BF16)],
        pieces,
        [VMEM] * ng,
        nbytes=1 << 20,
    )
    x = [columns[0]] + [swap(columns[p], "blk", nb, p) for p in range(1, nb)]
    if halves == 2:
        x += [swap(piece, "att", 2, 1) for piece in x]
    weights = call(
        functools.partial(weights_kernel, halves),
        sds((depth, 2 * hidden), BF16),
        (me, weight_scales[:, 0].astype(F32), weight_codes[:, 0]),
        [SMEM, SMEM, VMEM],
        nbytes=8 << 20,
    )
    partial = call(
        functools.partial(gate_up_kernel, nb, halves),
        [sds((rows, 2 * hidden), F32)] + [sds((rows, 2 * hidden), BF16)] * (nb - 1),
        (*x, weights),
        [VMEM] * (nb * halves + 1),
        flops=2 * nb * rows * depth * 2 * hidden,
        nbytes=3 << 20,
    )
    parts = [partial[0]] + [swap(partial[p], "blk", nb, p) for p in range(1, nb)]
    own = call(
        functools.partial(swiglu_kernel, nb),
        sds((rows, 2 * hidden), BF16),
        (*parts, cot),
        [VMEM] * (nb + 1),
        nbytes=1 << 20,
    )
    spread = call(
        functools.partial(spread_kernel, nb, halves),
        sds((2 * depth, 2 * nb * rows), BF16),
        (me, *x),
        [SMEM] + [VMEM] * (nb * halves),
        nbytes=8 << 20,
    )
    gathered = [own] + [swap(own, "blk", nb, p) for p in range(1, nb)]
    gradient = call(
        functools.partial(gradient_kernel, nb),
        sds((depth, 2, hidden), BF16),
        (*gathered, spread),
        [VMEM] * (nb + 1),
        scratch=[pltpu.VMEM((2 * nb * rows, hidden), BF16)],
        flops=4 * nb * rows * depth * 2 * hidden,
        nbytes=4 << 20,
    )
    return gradient[:, None]


def solution(mesh):
    return jax.shard_map(
        local,
        mesh=mesh,
        in_specs=(
            P(("group", "blk"), None),
            P(("group", "blk"), None),
            P(("group", "blk"), None, "att"),
            P("blk", "group", None, "att"),
            P("blk", "group", None, "att"),
        ),
        out_specs=P("blk", "group", None, "att"),
        check_vma=False,
    )
```

```python
import functools

import jax
import jax.numpy as jnp
from jax import lax
from jax.experimental import pallas as pl
from jax.experimental.pallas import tpu as pltpu
from jax.sharding import PartitionSpec as P

CAP = 16
BF16 = jnp.bfloat16
F32 = jnp.float32
VMEM_BYTES = 40 * 1024 * 1024
PACK_VMEM = 60 * 1024 * 1024


def call(kernel, out_shape, args, in_specs, out_specs=None, scratch=(), flops=0, nbytes=0, vmem_bytes=VMEM_BYTES):
    vmem = pl.BlockSpec(memory_space=pltpu.VMEM)
    return pl.pallas_call(
        kernel,
        out_shape=out_shape,
        in_specs=in_specs,
        out_specs=jax.tree.map(lambda _: vmem, out_shape) if out_specs is None else out_specs,
        scratch_shapes=scratch,
        compiler_params=pltpu.CompilerParams(vmem_limit_bytes=vmem_bytes),
        cost_estimate=pl.CostEstimate(flops=flops, bytes_accessed=nbytes, transcendentals=0),
    )(*args)


VMEM = pl.BlockSpec(memory_space=pltpu.VMEM)
SMEM = pl.BlockSpec(memory_space=pltpu.SMEM)
HBM = pl.BlockSpec(memory_space=pltpu.HBM)


def dot(a, b, dims=((1,), (0,))):
    return lax.dot_general(a, b, (dims, ((), ())), preferred_element_type=F32)


def iota(shape, dim):
    return lax.broadcasted_iota(jnp.int32, shape, dim)


def own_half(halves):
    return lax.axis_index("att") if halves == 2 else 0


def pack_kernel(ng, nb, halves, tokens, routed, act, *refs):
    outs, (token_buf, routed_buf, act_buf, sem) = refs[:ng], refs[ng:]
    top, count = routed.shape
    rows = ng * CAP
    width = tokens.shape[1] // (nb * halves)
    group, block, half = lax.axis_index("group"), lax.axis_index("blk"), own_half(halves)
    copies = [pltpu.make_async_copy(routed, routed_buf, sem.at[0])]
    copies.append(pltpu.make_async_copy(act, act_buf, sem.at[1]))
    for p in range(nb):
        start = pl.multiple_of(((block ^ p) * halves + half) * width, width)
        copies.append(
            pltpu.make_async_copy(tokens.at[:, pl.ds(start, width)], token_buf.at[p], sem.at[2 + p])
        )
    for copy in copies:
        copy.start()
    upto = (iota((count, count), 0) <= iota((count, count), 1)).astype(F32).astype(BF16)
    spread = (iota((count, count * top), 1) // top == iota((count, count * top), 0)).astype(F32).astype(BF16)
    own_slot = iota((top, count * top), 1) % top == iota((top, count * top), 0)
    slot = (iota((rows, count), 0) % CAP + 1).astype(F32)
    expert = (group ^ (iota((rows, 1), 0) // CAP)).astype(F32)
    copies[0].wait()
    ids = routed_buf[...]
    chosen = [jnp.sum((ids == (group ^ s)).astype(F32), axis=0, keepdims=True) for s in range(ng)]
    chosen_rows = jnp.concatenate([jnp.broadcast_to(c, (CAP, count)) for c in chosen], axis=0)
    place = dot(chosen_rows.astype(BF16), upto)
    selector = jnp.where(place == slot, chosen_rows, 0.0).astype(BF16)
    ids_wide = dot(ids.astype(F32).astype(BF16), spread)
    ids_flat = jnp.sum(jnp.where(own_slot, ids_wide, 0.0), axis=0, keepdims=True)
    pair = jnp.where(ids_flat == expert, dot(selector, spread), 0.0).astype(BF16)
    copies[1].wait()
    hidden = act.shape[2]
    cot = dot(pair, act_buf[...].reshape(count * top, hidden)).astype(BF16)
    for s in range(ng):
        outs[s][:, nb * width :] = cot[s * CAP : (s + 1) * CAP]
    for p in range(nb):
        copies[2 + p].wait()
        part = dot(selector, token_buf[p]).astype(BF16)
        for s in range(ng):
            outs[s][:, p * width : (p + 1) * width] = part[s * CAP : (s + 1) * CAP]


def regroup_kernel(ng, nb, width, *refs):
    pieces, outs = refs[:ng], refs[ng:]
    for s in range(ng):
        for p in range(nb):
            outs[p][s * CAP : (s + 1) * CAP, :] = pieces[s][:, p * width : (p + 1) * width]
        outs[nb][s * CAP : (s + 1) * CAP, :] = pieces[s][:, nb * width :]


def weights_kernel(halves, scales, codes, out):
    depth, _, hidden = codes.shape
    blocks, _, cols = scales.shape
    qrows, qcols = depth // blocks, hidden // cols
    half = own_half(halves)
    per_half = blocks // halves
    pick = [
        (iota((qrows, 2 * qrows), 1) == 2 * iota((qrows, 2 * qrows), 0) + j).astype(F32).astype(BF16)
        for j in range(2)
    ]
    for q in range(blocks):
        source = (q + half * per_half) % blocks if halves > 1 else q
        rows = codes[pl.ds(pl.multiple_of(source * qrows, qrows), qrows)].reshape(2 * qrows, hidden)
        for j in range(2):
            values = dot(pick[j], rows)
            for c in range(cols):
                at = j * hidden + c * qcols
                out[q * qrows : (q + 1) * qrows, at : at + qcols] = (
                    values[:, c * qcols : (c + 1) * qcols] * scales[source, j, c]
                ).astype(BF16)


def gate_up_kernel(nb, halves, *refs):
    pieces, weights, outs = refs[: nb * halves], refs[nb * halves], refs[nb * halves + 1 :]
    rows, width = pieces[0].shape
    for p in range(nb):
        total = dot(pieces[p][...], weights[:width])
        for h in range(1, halves):
            total += dot(pieces[h * nb + p][...], weights[h * width : (h + 1) * width])
        outs[p][...] = total.astype(outs[p].dtype)


def features_kernel(nb, halves, *refs):
    pieces, out = refs[: nb * halves], refs[nb * halves]
    rows, width = pieces[0].shape
    half = own_half(halves)
    for h in range(halves):
        start = pl.multiple_of((half ^ h) * width, width)
        for p in range(nb):
            out[p * rows : (p + 1) * rows, pl.ds(start, width)] = pieces[h * nb + p][...]


def swiglu_kernel(nb, *refs):
    parts, cot, out = refs[:nb], refs[nb], refs[nb + 1]
    hidden = cot.shape[1]
    total = parts[0][...]
    for p in range(1, nb):
        total += parts[p][...].astype(F32)
    gate, up = total[:, :hidden], total[:, hidden:]
    c = cot[...].astype(F32)
    s = jax.nn.sigmoid(gate)
    out[:, :hidden] = (c * up * s * (1.0 + gate * (1.0 - s))).astype(BF16)
    out[:, hidden:] = (c * gate * s).astype(BF16)


def gradient_kernel(nb, *refs):
    parts, features, out, stacked, buf, sem = refs[:nb], *refs[nb:]
    rows = parts[0].shape[0]
    depth, _, hidden = out.shape
    for p in range(nb):
        stacked[p * rows : (p + 1) * rows, :] = parts[p][...]
    step = min(128, depth)
    copies = []
    for k in range(depth // step):
        at = slice(k * step, (k + 1) * step)
        for j in range(2):
            buf[at, j, :] = dot(
                features[:, at], stacked[:, j * hidden : (j + 1) * hidden], ((0,), (0,))
            ).astype(BF16)
        copies.append(pltpu.make_async_copy(buf.at[at], out.at[at], sem.at[k]))
        copies[-1].start()
    for copy in copies:
        copy.wait()


def swap(x, axis, size, s):
    return lax.ppermute(x, axis, [(i, i ^ s) for i in range(size)])


def local(tokens, routed_experts, act_cotangent, weight_codes, weight_scales):
    ng, nb, na = lax.axis_size("group"), lax.axis_size("blk"), lax.axis_size("att")
    depth, _, _, hidden = weight_codes.shape
    halves = 2 if na == 2 and depth % 256 == 0 else 1
    width = depth // halves
    rows = ng * CAP
    sds = jax.ShapeDtypeStruct
    top, count = routed_experts.shape[1], tokens.shape[0]
    sent = call(
        functools.partial(pack_kernel, ng, nb, halves),
        [sds((CAP, nb * width + hidden), BF16)] * ng,
        (tokens, routed_experts.T, act_cotangent),
        [HBM, HBM, HBM],
        scratch=[
            pltpu.VMEM((nb, count, width), BF16),
            pltpu.VMEM((top, count), jnp.int32),
            pltpu.VMEM(act_cotangent.shape, BF16),
            pltpu.SemaphoreType.DMA((2 + nb,)),
        ],
        nbytes=2 << 20,
        vmem_bytes=PACK_VMEM,
    )
    codes, *sent = lax.optimization_barrier((weight_codes, *sent))
    weights = call(
        functools.partial(weights_kernel, halves),
        sds((depth, 2 * hidden), BF16),
        (weight_scales[:, 0].astype(F32), codes[:, 0]),
        [SMEM, VMEM],
        nbytes=4 << 20,
    )
    pieces = [sent[0]] + [swap(sent[s], "group", ng, s) for s in range(1, ng)]
    weights, *pieces = lax.optimization_barrier((weights, *pieces))
    *columns, cot = call(
        functools.partial(regroup_kernel, ng, nb, width),
        [sds((rows, width), BF16)] * nb + [sds((rows, hidden), BF16)],
        pieces,
        [VMEM] * ng,
        nbytes=1 << 20,
    )
    x = [columns[0]] + [swap(columns[p], "blk", nb, p) for p in range(1, nb)]
    if halves == 2:
        x += [swap(piece, "att", 2, 1) for piece in x]
    *partial, = call(
        functools.partial(gate_up_kernel, nb, halves),
        [sds((rows, 2 * hidden), F32)] + [sds((rows, 2 * hidden), BF16)] * (nb - 1),
        (*x, weights),
        [VMEM] * (nb * halves + 1),
        flops=2 * nb * rows * depth * 2 * hidden,
        nbytes=3 << 20,
    )
    *x, partial[1] = lax.optimization_barrier((*x, partial[1]))
    features = call(
        functools.partial(features_kernel, nb, halves),
        sds((nb * rows, depth), BF16),
        x,
        [VMEM] * (nb * halves),
        nbytes=3 << 20,
    )
    parts = [partial[0]] + [swap(partial[p], "blk", nb, p) for p in range(1, nb)]
    features, *parts = lax.optimization_barrier((features, *parts))
    own = call(
        functools.partial(swiglu_kernel, nb),
        sds((rows, 2 * hidden), BF16),
        (*parts, cot),
        [VMEM] * (nb + 1),
        nbytes=1 << 20,
    )
    gathered = [own] + [swap(own, "blk", nb, p) for p in range(1, nb)]
    step = min(128, depth)
    gradient = call(
        functools.partial(gradient_kernel, nb),
        sds((depth, 2, hidden), BF16),
        (*gathered, features),
        [VMEM] * (nb + 1),
        out_specs=HBM,
        scratch=[
            pltpu.VMEM((nb * rows, 2 * hidden), BF16),
            pltpu.VMEM((depth, 2, hidden), BF16),
            pltpu.SemaphoreType.DMA((depth // step,)),
        ],
        flops=2 * nb * rows * depth * 2 * hidden,
        nbytes=4 << 20,
    )
    return gradient[:, None]


def solution(mesh):
    return jax.shard_map(
        local,
        mesh=mesh,
        in_specs=(
            P(("group", "blk"), None),
            P(("group", "blk"), None),
            P(("group", "blk"), None, "att"),
            P("blk", "group", None, "att"),
            P("blk", "group", None, "att"),
        ),
        out_specs=P("blk", "group", None, "att"),
        check_vma=False,
    )
```

```python
import functools

import jax
import jax.numpy as jnp
from jax import lax
from jax.experimental import pallas as pl
from jax.experimental.pallas import tpu as pltpu
from jax.sharding import PartitionSpec as P

CAP = 16
BF16 = jnp.bfloat16
F32 = jnp.float32
VMEM_BYTES = 40 * 1024 * 1024
PACK_VMEM = 53 * 1024 * 1024


def call(kernel, out_shape, args, in_specs, out_specs=None, scratch=(), flops=0, nbytes=0, vmem_bytes=VMEM_BYTES):
    vmem = pl.BlockSpec(memory_space=pltpu.VMEM)
    return pl.pallas_call(
        kernel,
        out_shape=out_shape,
        in_specs=in_specs,
        out_specs=jax.tree.map(lambda _: vmem, out_shape) if out_specs is None else out_specs,
        scratch_shapes=scratch,
        compiler_params=pltpu.CompilerParams(vmem_limit_bytes=vmem_bytes),
        cost_estimate=pl.CostEstimate(flops=flops, bytes_accessed=nbytes, transcendentals=0),
    )(*args)


VMEM = pl.BlockSpec(memory_space=pltpu.VMEM)
SMEM = pl.BlockSpec(memory_space=pltpu.SMEM)
HBM = pl.BlockSpec(memory_space=pltpu.HBM)


def dot(a, b, dims=((1,), (0,))):
    return lax.dot_general(a, b, (dims, ((), ())), preferred_element_type=F32)


def iota(shape, dim):
    return lax.broadcasted_iota(jnp.int32, shape, dim)


def own_half(halves):
    return lax.axis_index("att") if halves == 2 else 0


def blk_partner(nb, halves, k):
    return jnp.where(lax.axis_index("att") == 0, k, nb - k) if halves == 2 and k else k


def group_partner(ng, k):
    return ng - k if k else 0


def pack_kernel(ng, nb, halves, tokens, routed, act, *refs):
    outs, (token_buf, routed_buf, act_buf, sem) = refs[:ng], refs[ng:]
    top, count = routed.shape
    rows = ng * CAP
    width = tokens.shape[1] // (nb * halves)
    group, block, half = lax.axis_index("group"), lax.axis_index("blk"), own_half(halves)
    copies = [pltpu.make_async_copy(routed, routed_buf, sem.at[0])]
    copies.append(pltpu.make_async_copy(act, act_buf, sem.at[1]))
    for p in range(nb):
        partner = block ^ blk_partner(nb, halves, p)
        start = pl.multiple_of((partner * halves + half) * width, width)
        copies.append(
            pltpu.make_async_copy(tokens.at[:, pl.ds(start, width)], token_buf.at[p], sem.at[2 + p])
        )
    for copy in copies:
        copy.start()
    upto = (iota((count, count), 0) <= iota((count, count), 1)).astype(F32).astype(BF16)
    spread = (iota((count, count * top), 1) // top == iota((count, count * top), 0)).astype(F32).astype(BF16)
    own_slot = iota((top, count * top), 1) % top == iota((top, count * top), 0)
    slot = (iota((rows, count), 0) % CAP + 1).astype(F32)
    slots = iota((rows, 1), 0) // CAP
    expert = (group ^ jnp.where(slots == 0, 0, ng - slots)).astype(F32)
    copies[0].wait()
    ids = routed_buf[...]
    chosen = [jnp.sum((ids == (group ^ group_partner(ng, s))).astype(F32), axis=0, keepdims=True) for s in range(ng)]
    chosen_rows = jnp.concatenate([jnp.broadcast_to(c, (CAP, count)) for c in chosen], axis=0)
    place = dot(chosen_rows.astype(BF16), upto)
    selector = jnp.where(place == slot, chosen_rows, 0.0).astype(BF16)
    ids_wide = dot(ids.astype(F32).astype(BF16), spread)
    ids_flat = jnp.sum(jnp.where(own_slot, ids_wide, 0.0), axis=0, keepdims=True)
    pair = jnp.where(ids_flat == expert, dot(selector, spread), 0.0).astype(BF16)
    copies[1].wait()
    hidden = act.shape[2]
    cot = dot(pair, act_buf[...].reshape(count * top, hidden)).astype(BF16)
    for s in range(ng):
        outs[s][:, nb * width :] = cot[s * CAP : (s + 1) * CAP]
    for p in range(nb):
        copies[2 + p].wait()
        part = dot(selector, token_buf[p]).astype(BF16)
        for s in range(ng):
            outs[s][:, p * width : (p + 1) * width] = part[s * CAP : (s + 1) * CAP]


def regroup_kernel(ng, nb, width, *refs):
    pieces, outs = refs[:ng], refs[ng:]
    for s in range(ng):
        for p in range(nb):
            outs[p][s * CAP : (s + 1) * CAP, :] = pieces[s][:, p * width : (p + 1) * width]
        outs[nb][s * CAP : (s + 1) * CAP, :] = pieces[s][:, nb * width :]


def weights_kernel(halves, scales, codes, out):
    depth, _, hidden = codes.shape
    blocks, _, cols = scales.shape
    qrows, qcols = depth // blocks, hidden // cols
    half = own_half(halves)
    per_half = blocks // halves
    pick = [
        (iota((qrows, 2 * qrows), 1) == 2 * iota((qrows, 2 * qrows), 0) + j).astype(F32).astype(BF16)
        for j in range(2)
    ]
    for q in range(blocks):
        source = (q + half * per_half) % blocks if halves > 1 else q
        rows = codes[pl.ds(pl.multiple_of(source * qrows, qrows), qrows)].reshape(2 * qrows, hidden)
        for j in range(2):
            values = dot(pick[j], rows)
            for c in range(cols):
                at = j * hidden + c * qcols
                out[q * qrows : (q + 1) * qrows, at : at + qcols] = (
                    values[:, c * qcols : (c + 1) * qcols] * scales[source, j, c]
                ).astype(BF16)


def gate_up_kernel(halves, *refs):
    pieces, weights, out = refs[:halves], refs[halves], refs[halves + 1]
    width = pieces[0].shape[1]
    total = dot(pieces[0][...], weights[:width])
    for h in range(1, halves):
        total += dot(pieces[h][...], weights[h * width : (h + 1) * width])
    out[...] = total.astype(out.dtype)


def features_kernel(nb, halves, *refs):
    pieces, out = refs[: nb * halves], refs[nb * halves]
    rows, width = pieces[0].shape
    half = own_half(halves)
    for h in range(halves):
        start = pl.multiple_of((half ^ h) * width, width)
        for p in range(nb):
            out[p * rows : (p + 1) * rows, pl.ds(start, width)] = pieces[h * nb + p][...]


def swiglu_kernel(nb, *refs):
    parts, cot, out = refs[:nb], refs[nb], refs[nb + 1]
    hidden = cot.shape[1]
    total = parts[0][...]
    for p in range(1, nb):
        total += parts[p][...].astype(F32)
    gate, up = total[:, :hidden], total[:, hidden:]
    c = cot[...].astype(F32)
    s = jax.nn.sigmoid(gate)
    out[:, :hidden] = (c * up * s * (1.0 + gate * (1.0 - s))).astype(BF16)
    out[:, hidden:] = (c * gate * s).astype(BF16)


def gradient_kernel(nb, *refs):
    parts, features, out, stacked, buf, sem = refs[:nb], *refs[nb:]
    rows = parts[0].shape[0]
    depth, _, hidden = out.shape
    for p in range(nb):
        stacked[p * rows : (p + 1) * rows, :] = parts[p][...]
    step = min(128, depth)
    copies = []
    for k in range(depth // step):
        at = slice(k * step, (k + 1) * step)
        for j in range(2):
            buf[at, j, :] = dot(
                features[:, at], stacked[:, j * hidden : (j + 1) * hidden], ((0,), (0,))
            ).astype(BF16)
        copies.append(pltpu.make_async_copy(buf.at[at], out.at[at], sem.at[k]))
        copies[-1].start()
    for copy in copies:
        copy.wait()


def swap_group(x, size, k):
    s = group_partner(size, k)
    return lax.ppermute(x, "group", [(i, i ^ s) for i in range(size)])


def swap_blk(x, size, halves, k):
    if halves == 1:
        return lax.ppermute(x, "blk", [(i, i ^ k) for i in range(size)])
    return lax.ppermute(
        x,
        ("blk", "att"),
        [(2 * i + c, 2 * (i ^ s) + c) for i in range(size) for c, s in ((0, k), (1, size - k))],
    )


def swap_att(x):
    return lax.ppermute(x, "att", [(0, 1), (1, 0)])


def local(tokens, routed_experts, act_cotangent, weight_codes, weight_scales):
    ng, nb, na = lax.axis_size("group"), lax.axis_size("blk"), lax.axis_size("att")
    depth, _, _, hidden = weight_codes.shape
    halves = 2 if na == 2 and depth % 256 == 0 else 1
    width = depth // halves
    rows = ng * CAP
    sds = jax.ShapeDtypeStruct
    top, count = routed_experts.shape[1], tokens.shape[0]
    sent = call(
        functools.partial(pack_kernel, ng, nb, halves),
        [sds((CAP, nb * width + hidden), BF16)] * ng,
        (tokens, routed_experts.T, act_cotangent),
        [HBM, HBM, HBM],
        scratch=[
            pltpu.VMEM((nb, count, width), BF16),
            pltpu.VMEM((top, count), jnp.int32),
            pltpu.VMEM(act_cotangent.shape, BF16),
            pltpu.SemaphoreType.DMA((2 + nb,)),
        ],
        nbytes=2 << 20,
        vmem_bytes=PACK_VMEM,
    )
    codes, *sent = lax.optimization_barrier((weight_codes, *sent))
    weights = call(
        functools.partial(weights_kernel, halves),
        sds((depth, 2 * hidden), BF16),
        (weight_scales[:, 0].astype(F32), codes[:, 0]),
        [SMEM, VMEM],
        nbytes=4 << 20,
    )
    pieces = [sent[0]] + [swap_group(sent[s], ng, s) for s in range(1, ng)]
    weights, *pieces = lax.optimization_barrier((weights, *pieces))
    *columns, cot = call(
        functools.partial(regroup_kernel, ng, nb, width),
        [sds((rows, width), BF16)] * nb + [sds((rows, hidden), BF16)],
        pieces,
        [VMEM] * ng,
        nbytes=1 << 20,
    )
    x = [columns[0]] + [swap_blk(columns[p], nb, halves, p) for p in range(1, nb)]
    if halves == 2:
        other = [swap_att(piece) for piece in x]
        x += [other[0], *other[:0:-1]]
    partial = [
        call(
            functools.partial(gate_up_kernel, halves),
            sds((rows, 2 * hidden), BF16 if p else F32),
            (*x[p::nb], weights),
            [VMEM] * (halves + 1),
            flops=2 * rows * depth * 2 * hidden,
            nbytes=1 << 20,
        )
        for p in range(nb)
    ]
    parts = [partial[0]] + [swap_blk(partial[p], nb, halves, p) for p in range(1, nb)]
    features = call(
        functools.partial(features_kernel, nb, halves),
        sds((nb * rows, depth), BF16),
        [piece for h in range(halves) for piece in (x[h * nb], *x[(h + 1) * nb - 1 : h * nb : -1])],
        [VMEM] * (nb * halves),
        nbytes=3 << 20,
    )
    features, *parts = lax.optimization_barrier((features, *parts))
    own = call(
        functools.partial(swiglu_kernel, nb),
        sds((rows, 2 * hidden), BF16),
        (*parts, cot),
        [VMEM] * (nb + 1),
        nbytes=1 << 20,
    )
    gathered = [own] + [swap_blk(own, nb, halves, p) for p in range(nb - 1, 0, -1)]
    step = min(128, depth)
    gradient = call(
        functools.partial(gradient_kernel, nb),
        sds((depth, 2, hidden), BF16),
        (*gathered, features),
        [VMEM] * (nb + 1),
        out_specs=HBM,
        scratch=[
            pltpu.VMEM((nb * rows, 2 * hidden), BF16),
            pltpu.VMEM((depth, 2, hidden), BF16),
            pltpu.SemaphoreType.DMA((depth // step,)),
        ],
        flops=2 * nb * rows * depth * 2 * hidden,
        nbytes=4 << 20,
    )
    return gradient[:, None]


def solution(mesh):
    return jax.shard_map(
        local,
        mesh=mesh,
        in_specs=(
            P(("group", "blk"), None),
            P(("group", "blk"), None),
            P(("group", "blk"), None, "att"),
            P("blk", "group", None, "att"),
            P("blk", "group", None, "att"),
        ),
        out_specs=P("blk", "group", None, "att"),
        check_vma=False,
    )
```

```python
import functools

import jax
import jax.numpy as jnp
from jax import lax
from jax.experimental import pallas as pl
from jax.experimental.pallas import tpu as pltpu
from jax.sharding import PartitionSpec as P

CAP = 16
BF16 = jnp.bfloat16
F32 = jnp.float32
VMEM_BYTES = 40 * 1024 * 1024
PAIRED_CUTS = (1, 2)
PACK_VMEM = 53 * 1024 * 1024


def call(kernel, out_shape, args, in_specs, out_specs=None, scratch=(), flops=0, nbytes=0, vmem_bytes=VMEM_BYTES, aliases=None):
    vmem = pl.BlockSpec(memory_space=pltpu.VMEM)
    return pl.pallas_call(
        kernel,
        out_shape=out_shape,
        in_specs=in_specs,
        out_specs=jax.tree.map(lambda _: vmem, out_shape) if out_specs is None else out_specs,
        scratch_shapes=scratch,
        input_output_aliases=aliases or {},
        compiler_params=pltpu.CompilerParams(vmem_limit_bytes=vmem_bytes),
        cost_estimate=pl.CostEstimate(flops=flops, bytes_accessed=nbytes, transcendentals=0),
    )(*args)


VMEM = pl.BlockSpec(memory_space=pltpu.VMEM)
SMEM = pl.BlockSpec(memory_space=pltpu.SMEM)
HBM = pl.BlockSpec(memory_space=pltpu.HBM)


def dot(a, b, dims=((1,), (0,))):
    return lax.dot_general(a, b, (dims, ((), ())), preferred_element_type=F32)


def iota(shape, dim):
    return lax.broadcasted_iota(jnp.int32, shape, dim)


def own_half(halves):
    return lax.axis_index("att") if halves == 2 else 0


def group_partner(ng, k):
    return ng - k if k else 0


def pack_kernel(ng, nb, halves, tokens, routed, act, *refs):
    outs, (token_buf, routed_buf, act_buf, sem) = refs[:ng], refs[ng:]
    top, count = routed.shape
    rows = ng * CAP
    width = tokens.shape[1] // (nb * halves)
    group, block, half = lax.axis_index("group"), lax.axis_index("blk"), own_half(halves)
    copies = [pltpu.make_async_copy(routed, routed_buf, sem.at[0])]
    copies.append(pltpu.make_async_copy(act, act_buf, sem.at[1]))
    for p in range(nb):
        partner = block ^ p
        start = pl.multiple_of((partner * halves + half) * width, width)
        copies.append(
            pltpu.make_async_copy(tokens.at[:, pl.ds(start, width)], token_buf.at[p], sem.at[2 + p])
        )
    for copy in copies:
        copy.start()
    upto = (iota((count, count), 0) <= iota((count, count), 1)).astype(F32).astype(BF16)
    spread = (iota((count, count * top), 1) // top == iota((count, count * top), 0)).astype(F32).astype(BF16)
    own_slot = iota((top, count * top), 1) % top == iota((top, count * top), 0)
    slot = (iota((rows, count), 0) % CAP + 1).astype(F32)
    slots = iota((rows, 1), 0) // CAP
    expert = (group ^ jnp.where(slots == 0, 0, ng - slots)).astype(F32)
    copies[0].wait()
    ids = routed_buf[...]
    chosen = [jnp.sum((ids == (group ^ group_partner(ng, s))).astype(F32), axis=0, keepdims=True) for s in range(ng)]
    chosen_rows = jnp.concatenate([jnp.broadcast_to(c, (CAP, count)) for c in chosen], axis=0)
    place = dot(chosen_rows.astype(BF16), upto)
    selector = jnp.where(place == slot, chosen_rows, 0.0).astype(BF16)
    ids_wide = dot(ids.astype(F32).astype(BF16), spread)
    ids_flat = jnp.sum(jnp.where(own_slot, ids_wide, 0.0), axis=0, keepdims=True)
    pair = jnp.where(ids_flat == expert, dot(selector, spread), 0.0).astype(BF16)
    copies[1].wait()
    hidden = act.shape[2]
    cot = dot(pair, act_buf[...].reshape(count * top, hidden)).astype(BF16)
    for s in range(ng):
        outs[s][:, nb * width :] = cot[s * CAP : (s + 1) * CAP]
    for p in range(nb):
        copies[2 + p].wait()
        part = dot(selector, token_buf[p]).astype(BF16)
        for s in range(ng):
            outs[s][:, p * width : (p + 1) * width] = part[s * CAP : (s + 1) * CAP]


def regroup_kernel(ng, nb, width, with_cot, *refs):
    pieces, outs = refs[:ng], refs[ng:]
    for s in range(ng):
        at = slice(s * CAP, (s + 1) * CAP)
        cot = pieces[s][:, nb * width :]
        for p in range(nb):
            outs[p][at, :width] = pieces[s][:, p * width : (p + 1) * width]
            if p in with_cot:
                outs[p][at, width:] = cot
        outs[nb][at, :] = cot


def weights_kernel(halves, scales, codes, out):
    depth, _, hidden = codes.shape
    blocks, _, cols = scales.shape
    qrows, qcols = depth // blocks, hidden // cols
    half = own_half(halves)
    per_half = blocks // halves
    pick = [
        (iota((qrows, 2 * qrows), 1) == 2 * iota((qrows, 2 * qrows), 0) + j).astype(F32).astype(BF16)
        for j in range(2)
    ]
    for q in range(blocks):
        source = (q + half * per_half) % blocks if halves > 1 else q
        rows = codes[pl.ds(pl.multiple_of(source * qrows, qrows), qrows)].reshape(2 * qrows, hidden)
        for j in range(2):
            values = dot(pick[j], rows)
            for c in range(cols):
                at = (2 * c + j) * qcols
                out[q * qrows : (q + 1) * qrows, at : at + qcols] = (
                    values[:, c * qcols : (c + 1) * qcols] * scales[source, j, c]
                ).astype(BF16)


def gate_up_kernel(halves, at, *refs):
    blocks, weights, out = refs[:-2], refs[-2], refs[-1]
    rows, width = blocks[0].shape[0], weights.shape[0] // halves
    cols = slice(at, at + out.shape[1])
    for i in range(len(blocks) // halves):
        total = dot(blocks[halves * i][:, :width], weights[:width, cols])
        for h in range(1, halves):
            total += dot(blocks[halves * i + h][:, :width], weights[h * width : (h + 1) * width, cols])
        out[i * rows : (i + 1) * rows, :] = total.astype(out.dtype)


def features_kernel(halves, *refs):
    blocks, out = refs[:-1], refs[-1]
    rows, width = blocks[0].shape[0], out.shape[1] // halves
    half = own_half(halves)
    for i in range(len(blocks) // halves):
        for h in range(halves):
            start = pl.multiple_of((half ^ h) * width, width)
            out[i * rows : (i + 1) * rows, pl.ds(start, width)] = blocks[halves * i + h][:, :width]


def add_kernel(kept, arrived, out):
    out[...] = (kept[...] + arrived[...].astype(F32)).astype(BF16)


def swiglu(total, cot, out):
    size = cot.shape[1]
    gate, up = total[:, :size], total[:, size:]
    c = cot.astype(F32)
    s = jax.nn.sigmoid(gate)
    out[:, :size] = (c * up * s * (1.0 + gate * (1.0 - s))).astype(BF16)
    out[:, size:] = (c * gate * s).astype(BF16)


def pair_swiglu_kernel(at, size, kept, near, far, cot, far_columns, out):
    rows, hidden = cot.shape
    total = kept[...] + near[...].astype(F32)
    total += jnp.concatenate([far[rows:, :], far[:rows, :]], axis=0).astype(F32)
    skip = far_columns.shape[1] - hidden
    for c in range(out.shape[1] // (2 * size)):
        cols = slice(2 * c * size, 2 * (c + 1) * size)
        h = at + c * size
        cots = [cot[:, h : h + size], far_columns[:, skip + h : skip + h + size]]
        swiglu(total[:, cols], jnp.concatenate(cots, axis=0), out.at[:, cols])


def swiglu_kernel(size, *refs):
    parts, cot, out = refs[:-2], refs[-2], refs[-1]
    total = parts[0][...]
    for part in parts[1:]:
        total += part[...].astype(F32)
    for c in range(cot.shape[1] // size):
        cols = slice(2 * c * size, 2 * (c + 1) * size)
        swiglu(total[:, cols], cot[:, c * size : (c + 1) * size], out.at[:, cols])


def gradient_chunk(parts, features, size, stacked, rows, out, written):
    count, depth = parts[0].shape[0], features.shape[1]
    for i, part in enumerate(parts):
        stacked[i * count : (i + 1) * count, :] = part[...]
    step = min(128, depth)
    for k in range(depth // step):
        d = slice(k * step, (k + 1) * step)
        values = dot(features[:, d], stacked[...], ((0,), (0,)))
        for c in range(stacked.shape[1] // (2 * size)):
            for j in range(2):
                at = (2 * c + j) * size
                rows[c, pl.ds(2 * k * step + j, step, stride=2), :] = values[:, at : at + size]
            both = rows[c, 2 * k * step : 2 * (k + 1) * step, :].astype(BF16)
            out[d, :, c * size : (c + 1) * size] = both.reshape(step, 2, size)
        written(k, d)


def chunk_kernel(at, size, first, *refs):
    *parts, features, out, stacked, rows = refs if first else refs[1:]
    out = out.at[:, :, at : at + stacked.shape[1] // 2]
    gradient_chunk(parts, features, size, stacked, rows, out, lambda k, d: None)


def gradient_kernel(at, size, *refs):
    finished, (*parts, features, out, stacked, rows, buf, sem) = refs[: at > 0], refs[at > 0 :]
    whole = finished[0] if finished else buf
    copies = []

    def copy(k, d):
        copies.append(pltpu.make_async_copy(whole.at[d], out.at[d], sem.at[k]))
        copies[-1].start()

    gradient_chunk(parts, features, size, stacked, rows, whole.at[:, :, at:], copy)
    for item in copies:
        item.wait()


def swap_group(x, size, k):
    s = group_partner(size, k)
    return lax.ppermute(x, "group", [(i, i ^ s) for i in range(size)])


def swap_blk(x, size, p):
    return lax.ppermute(x, "blk", [(i, i ^ p) for i in range(size)])


def swap_att(x):
    return lax.ppermute(x, "att", [(0, 1), (1, 0)])


def local(tokens, routed_experts, act_cotangent, weight_codes, weight_scales):
    ng, nb, na = lax.axis_size("group"), lax.axis_size("blk"), lax.axis_size("att")
    depth, _, _, hidden = weight_codes.shape
    halves = 2 if na == 2 and depth % 256 == 0 else 1
    width = depth // halves
    rows = ng * CAP
    sds = jax.ShapeDtypeStruct
    top, count = routed_experts.shape[1], tokens.shape[0]
    sent = call(
        functools.partial(pack_kernel, ng, nb, halves),
        [sds((CAP, nb * width + hidden), BF16)] * ng,
        (tokens, routed_experts.T, act_cotangent),
        [HBM, HBM, HBM],
        scratch=[
            pltpu.VMEM((nb, count, width), BF16),
            pltpu.VMEM((top, count), jnp.int32),
            pltpu.VMEM(act_cotangent.shape, BF16),
            pltpu.SemaphoreType.DMA((2 + nb,)),
        ],
        nbytes=2 << 20,
        vmem_bytes=PACK_VMEM,
    )
    codes, *sent = lax.optimization_barrier((weight_codes, *sent))
    weights = call(
        functools.partial(weights_kernel, halves),
        sds((depth, 2 * hidden), BF16),
        (weight_scales[:, 0].astype(F32), codes[:, 0]),
        [SMEM, VMEM],
        nbytes=4 << 20,
    )
    pieces = [sent[0]] + [swap_group(sent[s], ng, s) for s in range(1, ng)]
    weights, *pieces = lax.optimization_barrier((weights, *pieces))
    paired = halves == 2 and nb == 4
    with_cot = (3,) if paired else ()
    *columns, cot = call(
        functools.partial(regroup_kernel, ng, nb, width, with_cot),
        [sds((rows, width + hidden * (p in with_cot)), BF16) for p in range(nb)] + [sds((rows, hidden), BF16)],
        pieces,
        [VMEM] * ng,
        nbytes=1 << 20,
    )
    size = hidden // weight_scales.shape[3]
    x = {0: [columns[0]]} | {p: [swap_blk(columns[p], nb, p)] for p in range(1, nb)}
    if halves == 2:
        x = {p: [piece, swap_att(piece)] for p, (piece,) in x.items()}

    def gate_up(blocks, at, to, dtype):
        return call(
            functools.partial(gate_up_kernel, halves, 2 * at),
            sds((len(blocks) * rows, 2 * (to - at)), dtype),
            (*(piece for p in blocks for piece in x[p]), weights),
            [VMEM] * (len(blocks) * halves + 1),
            nbytes=1 << 20,
        )

    block_order = (0, 3, 1, 2) if paired else tuple(range(nb))
    if paired:
        cuts = [0, *(size * c for c in PAIRED_CUTS if size * c < hidden), hidden]
        chunks = list(zip(cuts[:-1], cuts[1:]))
        away = [gate_up((1, 2), *chunk, BF16) for chunk in chunks]
        features = call(
            functools.partial(features_kernel, halves),
            sds((nb * rows, depth), BF16),
            [piece for p in block_order for piece in x[p]],
            [VMEM] * (nb * halves),
            nbytes=3 << 20,
        )
        kept = [gate_up((0, 3), *chunk, F32) for chunk in chunks]
        near = [swap_blk(a, nb, 1) for a in away]
        pair = [
            call(add_kernel, sds(k.shape, BF16), (k, n), [VMEM] * 2, nbytes=1 << 18)
            for k, n in zip(kept, near)
        ]
        far = [swap_blk(p, nb, 3) for p in pair]
        own = [
            call(
                functools.partial(pair_swiglu_kernel, at, size),
                sds((2 * rows, 2 * (to - at)), BF16),
                (kept[c], near[c], far[c], cot, x[3][0]),
                [VMEM] * 5,
                nbytes=1 << 18,
            )
            for c, (at, to) in enumerate(chunks)
        ]
        parts = [[o, swap_blk(o, nb, 1)] for o in own]
    else:
        chunks = [(0, hidden)]
        features = call(
            functools.partial(features_kernel, halves),
            sds((nb * rows, depth), BF16),
            [piece for p in block_order for piece in x[p]],
            [VMEM] * (nb * halves),
            nbytes=3 << 20,
        )
        partial = [gate_up((p,), 0, hidden, BF16 if p else F32) for p in range(nb)]
        own = call(
            functools.partial(swiglu_kernel, size),
            sds((rows, 2 * hidden), BF16),
            (partial[0], *(swap_blk(partial[p], nb, p) for p in range(1, nb)), cot),
            [VMEM] * (nb + 1),
            nbytes=1 << 20,
        )
        parts = [[own] + [swap_blk(own, nb, p) for p in range(1, nb)]]

    def buffers(at, to):
        return [
            pltpu.VMEM((nb * rows, 2 * (to - at)), BF16),
            pltpu.VMEM(((to - at) // size, 2 * depth, size), F32),
        ]

    finished = []
    for (at, to), part in zip(chunks[:-1], parts):
        finished = [
            call(
                functools.partial(chunk_kernel, at, size, not finished),
                sds((depth, 2, hidden), BF16),
                (*finished, *part, features),
                [VMEM] * (len(finished) + len(part) + 1),
                scratch=buffers(at, to),
                nbytes=1 << 20,
                aliases={0: 0} if finished else {},
            )
        ]
    at, to = chunks[-1]
    step = min(128, depth)
    gradient = call(
        functools.partial(gradient_kernel, at, size),
        sds((depth, 2, hidden), BF16),
        (*finished, *parts[-1], features),
        [VMEM] * (len(finished) + len(parts[-1]) + 1),
        out_specs=HBM,
        scratch=[
            *buffers(at, to),
            pltpu.VMEM((16, 2, 128) if finished else (depth, 2, hidden), BF16),
            pltpu.SemaphoreType.DMA((depth // step,)),
        ],
        nbytes=4 << 20,
    )
    return gradient[:, None]


def solution(mesh):
    return jax.shard_map(
        local,
        mesh=mesh,
        in_specs=(
            P(("group", "blk"), None),
            P(("group", "blk"), None),
            P(("group", "blk"), None, "att"),
            P("blk", "group", None, "att"),
            P("blk", "group", None, "att"),
        ),
        out_specs=P("blk", "group", None, "att"),
        check_vma=False,
    )
```

```python
import functools

import jax
import jax.numpy as jnp
from jax import lax
from jax.experimental import pallas as pl
from jax.experimental.pallas import tpu as pltpu
from jax.sharding import PartitionSpec as P

CAP = 16
BF16 = jnp.bfloat16
F32 = jnp.float32
VMEM_BYTES = 40 * 1024 * 1024
PAIRED_CUTS = (1, 2)


def call(kernel, out_shape, args, in_specs, out_specs=None, scratch=(), flops=0, nbytes=0, aliases=None):
    vmem = pl.BlockSpec(memory_space=pltpu.VMEM)
    return pl.pallas_call(
        kernel,
        out_shape=out_shape,
        in_specs=in_specs,
        out_specs=jax.tree.map(lambda _: vmem, out_shape) if out_specs is None else out_specs,
        scratch_shapes=scratch,
        input_output_aliases=aliases or {},
        compiler_params=pltpu.CompilerParams(vmem_limit_bytes=VMEM_BYTES),
        cost_estimate=pl.CostEstimate(flops=flops, bytes_accessed=nbytes, transcendentals=0),
    )(*args)


VMEM = pl.BlockSpec(memory_space=pltpu.VMEM)
SMEM = pl.BlockSpec(memory_space=pltpu.SMEM)
HBM = pl.BlockSpec(memory_space=pltpu.HBM)


def dot(a, b, dims=((1,), (0,))):
    return lax.dot_general(a, b, (dims, ((), ())), preferred_element_type=F32)


def iota(shape, dim):
    return lax.broadcasted_iota(jnp.int32, shape, dim)


def own_half(halves):
    return lax.axis_index("att") if halves == 2 else 0


def group_partner(ng, k):
    return ng - k if k else 0


def pack_kernel(ng, nb, halves, tokens, routed, act, *refs):
    outs, (token_buf, routed_buf, act_buf, sem) = refs[:ng], refs[ng:]
    top, count = routed.shape
    rows = ng * CAP
    width = tokens.shape[1] // (nb * halves)
    group, block, half = lax.axis_index("group"), lax.axis_index("blk"), own_half(halves)
    copies = [pltpu.make_async_copy(routed, routed_buf, sem.at[0])]
    for p in range(nb):
        partner = block ^ p
        start = pl.multiple_of((partner * halves + half) * width, width)
        copies.append(
            pltpu.make_async_copy(tokens.at[:, pl.ds(start, width)], token_buf.at[p], sem.at[1 + p])
        )
    first = len(copies)
    size = count // 4
    for k in range(4):
        at = pl.ds(k * size, size)
        copies.append(pltpu.make_async_copy(act.at[at], act_buf.at[at], sem.at[first + k]))
    for copy in copies:
        copy.start()
    upto = (iota((count, count), 0) <= iota((count, count), 1)).astype(F32).astype(BF16)
    spread = (iota((count, count * top), 1) // top == iota((count, count * top), 0)).astype(F32).astype(BF16)
    own_slot = iota((top, count * top), 1) % top == iota((top, count * top), 0)
    slot = (iota((rows, count), 0) % CAP + 1).astype(F32)
    slots = iota((rows, 1), 0) // CAP
    expert = (group ^ jnp.where(slots == 0, 0, ng - slots)).astype(F32)
    copies[0].wait()
    ids = routed_buf[...]
    chosen = [jnp.sum((ids == (group ^ group_partner(ng, s))).astype(F32), axis=0, keepdims=True) for s in range(ng)]
    chosen_rows = jnp.concatenate([jnp.broadcast_to(c, (CAP, count)) for c in chosen], axis=0)
    place = dot(chosen_rows.astype(BF16), upto)
    selector = jnp.where(place == slot, chosen_rows, 0.0).astype(BF16)
    ids_wide = dot(ids.astype(F32).astype(BF16), spread)
    ids_flat = jnp.sum(jnp.where(own_slot, ids_wide, 0.0), axis=0, keepdims=True)
    pair = jnp.where(ids_flat == expert, dot(selector, spread), 0.0).astype(BF16)
    for p in range(nb):
        copies[1 + p].wait()
        part = dot(selector, token_buf[p]).astype(BF16)
        for s in range(ng):
            outs[s][:, p * width : (p + 1) * width] = part[s * CAP : (s + 1) * CAP]
    for copy in copies[first:]:
        copy.wait()
    hidden = act.shape[2]
    cot = dot(pair, act_buf[...].reshape(count * top, hidden)).astype(BF16)
    for s in range(ng):
        outs[s][:, nb * width :] = cot[s * CAP : (s + 1) * CAP]


def regroup_kernel(ng, nb, width, with_cot, *refs):
    pieces, outs = refs[:ng], refs[ng:]
    for s in range(ng):
        at = slice(s * CAP, (s + 1) * CAP)
        cot = pieces[s][:, nb * width :]
        for p in range(nb):
            outs[p][at, :width] = pieces[s][:, p * width : (p + 1) * width]
            if p in with_cot:
                outs[p][at, width:] = cot
        outs[nb][at, :] = cot


def weights_kernel(halves, scales, codes_hbm, out, codes, sem):
    depth, _, hidden = codes.shape
    blocks, _, cols = scales.shape
    qrows, qcols = depth // blocks, hidden // cols
    copies = [
        pltpu.make_async_copy(codes_hbm.at[at], codes.at[at], sem.at[q])
        for q, at in enumerate(pl.ds(q * qrows, qrows) for q in range(blocks))
    ]
    for copy in copies:
        copy.start()
    half = own_half(halves)
    per_half = blocks // halves
    pick = [
        (iota((qrows, 2 * qrows), 1) == 2 * iota((qrows, 2 * qrows), 0) + j).astype(F32).astype(BF16)
        for j in range(2)
    ]
    for copy in copies:
        copy.wait()
    for q in range(blocks):
        source = (q + half * per_half) % blocks if halves > 1 else q
        rows = codes[pl.ds(pl.multiple_of(source * qrows, qrows), qrows)].reshape(2 * qrows, hidden)
        for j in range(2):
            values = dot(pick[j], rows)
            for c in range(cols):
                at = (2 * c + j) * qcols
                out[q * qrows : (q + 1) * qrows, at : at + qcols] = (
                    values[:, c * qcols : (c + 1) * qcols] * scales[source, j, c]
                ).astype(BF16)


def gate_up_kernel(halves, at, *refs):
    blocks, weights, out = refs[:-2], refs[-2], refs[-1]
    rows, width = blocks[0].shape[0], weights.shape[0] // halves
    cols = slice(at, at + out.shape[1])
    for i in range(len(blocks) // halves):
        total = dot(blocks[halves * i][:, :width], weights[:width, cols])
        for h in range(1, halves):
            total += dot(blocks[halves * i + h][:, :width], weights[h * width : (h + 1) * width, cols])
        out[i * rows : (i + 1) * rows, :] = total.astype(out.dtype)


def features_kernel(halves, *refs):
    blocks, out = refs[:-1], refs[-1]
    rows, width = blocks[0].shape[0], out.shape[1] // halves
    half = own_half(halves)
    for i in range(len(blocks) // halves):
        for h in range(halves):
            start = pl.multiple_of((half ^ h) * width, width)
            out[i * rows : (i + 1) * rows, pl.ds(start, width)] = blocks[halves * i + h][:, :width]


def add_kernel(kept, arrived, out):
    out[...] = (kept[...] + arrived[...].astype(F32)).astype(BF16)


def swiglu(total, cot, out):
    size = cot.shape[1]
    gate, up = total[:, :size], total[:, size:]
    c = cot.astype(F32)
    s = jax.nn.sigmoid(gate)
    out[:, :size] = (c * up * s * (1.0 + gate * (1.0 - s))).astype(BF16)
    out[:, size:] = (c * gate * s).astype(BF16)


def pair_swiglu_kernel(at, size, kept, near, far, cot, far_columns, out):
    rows, hidden = cot.shape
    total = kept[...] + near[...].astype(F32)
    total += jnp.concatenate([far[rows:, :], far[:rows, :]], axis=0).astype(F32)
    skip = far_columns.shape[1] - hidden
    for c in range(out.shape[1] // (2 * size)):
        cols = slice(2 * c * size, 2 * (c + 1) * size)
        h = at + c * size
        cots = [cot[:, h : h + size], far_columns[:, skip + h : skip + h + size]]
        swiglu(total[:, cols], jnp.concatenate(cots, axis=0), out.at[:, cols])


def swiglu_kernel(size, *refs):
    parts, cot, out = refs[:-2], refs[-2], refs[-1]
    total = parts[0][...]
    for part in parts[1:]:
        total += part[...].astype(F32)
    for c in range(cot.shape[1] // size):
        cols = slice(2 * c * size, 2 * (c + 1) * size)
        swiglu(total[:, cols], cot[:, c * size : (c + 1) * size], out.at[:, cols])


def gradient_chunk(parts, features, size, stacked, rows, out, written):
    count, depth = parts[0].shape[0], features.shape[1]
    for i, part in enumerate(parts):
        stacked[i * count : (i + 1) * count, :] = part[...]
    step = min(128, depth)
    for k in range(depth // step):
        d = slice(k * step, (k + 1) * step)
        values = dot(features[:, d], stacked[...], ((0,), (0,)))
        for c in range(stacked.shape[1] // (2 * size)):
            for j in range(2):
                at = (2 * c + j) * size
                rows[c, pl.ds(2 * k * step + j, step, stride=2), :] = values[:, at : at + size]
            both = rows[c, 2 * k * step : 2 * (k + 1) * step, :].astype(BF16)
            out[d, :, c * size : (c + 1) * size] = both.reshape(step, 2, size)
        written(k, d)


def chunk_kernel(at, size, first, *refs):
    *parts, features, out, stacked, rows = refs if first else refs[1:]
    out = out.at[:, :, at : at + stacked.shape[1] // 2]
    gradient_chunk(parts, features, size, stacked, rows, out, lambda k, d: None)


def gradient_kernel(at, size, *refs):
    finished, (*parts, features, out, stacked, rows, buf, sem) = refs[: at > 0], refs[at > 0 :]
    whole = finished[0] if finished else buf
    copies = []

    def copy(k, d):
        copies.append(pltpu.make_async_copy(whole.at[d], out.at[d], sem.at[k]))
        copies[-1].start()

    gradient_chunk(parts, features, size, stacked, rows, whole.at[:, :, at:], copy)
    for item in copies:
        item.wait()


def swap_group(x, size, k):
    s = group_partner(size, k)
    return lax.ppermute(x, "group", [(i, i ^ s) for i in range(size)])


def swap_blk(x, size, p):
    return lax.ppermute(x, "blk", [(i, i ^ p) for i in range(size)])


def swap_att(x):
    return lax.ppermute(x, "att", [(0, 1), (1, 0)])


def local(tokens, routed_experts, act_cotangent, weight_codes, weight_scales):
    ng, nb, na = lax.axis_size("group"), lax.axis_size("blk"), lax.axis_size("att")
    depth, _, _, hidden = weight_codes.shape
    halves = 2 if na == 2 and depth % 256 == 0 else 1
    width = depth // halves
    rows = ng * CAP
    sds = jax.ShapeDtypeStruct
    top, count = routed_experts.shape[1], tokens.shape[0]
    sent = call(
        functools.partial(pack_kernel, ng, nb, halves),
        [sds((CAP, nb * width + hidden), BF16)] * ng,
        [pltpu.with_memory_space_constraint(a, pltpu.HBM) for a in (tokens, routed_experts.T, act_cotangent)],
        [HBM, HBM, HBM],
        scratch=[
            pltpu.VMEM((nb, count, width), BF16),
            pltpu.VMEM((top, count), jnp.int32),
            pltpu.VMEM(act_cotangent.shape, BF16),
            pltpu.SemaphoreType.DMA((5 + nb,)),
        ],
        nbytes=2 << 20,
    )
    codes, *sent = lax.optimization_barrier((weight_codes, *sent))
    weights = call(
        functools.partial(weights_kernel, halves),
        sds((depth, 2 * hidden), BF16),
        (weight_scales[:, 0].astype(F32), pltpu.with_memory_space_constraint(codes[:, 0], pltpu.HBM)),
        [SMEM, HBM],
        scratch=[
            pltpu.VMEM((depth, 2, hidden), BF16),
            pltpu.SemaphoreType.DMA((weight_scales.shape[0],)),
        ],
        nbytes=4 << 20,
    )
    pieces = [sent[0]] + [swap_group(sent[s], ng, s) for s in range(1, ng)]
    weights, *pieces = lax.optimization_barrier((weights, *pieces))
    paired = halves == 2 and nb == 4
    with_cot = ()
    *columns, cot = call(
        functools.partial(regroup_kernel, ng, nb, width, with_cot),
        [sds((rows, width + hidden * (p in with_cot)), BF16) for p in range(nb)] + [sds((rows, hidden), BF16)],
        pieces,
        [VMEM] * ng,
        nbytes=1 << 20,
    )
    size = hidden // weight_scales.shape[3]
    x = {0: [columns[0]]} | {p: [swap_blk(columns[p], nb, p)] for p in range(1, nb)}
    if halves == 2:
        x = {p: [piece, swap_att(piece)] for p, (piece,) in x.items()}

    def gate_up(blocks, at, to, dtype):
        return call(
            functools.partial(gate_up_kernel, halves, 2 * at),
            sds((len(blocks) * rows, 2 * (to - at)), dtype),
            (*(piece for p in blocks for piece in x[p]), weights),
            [VMEM] * (len(blocks) * halves + 1),
            nbytes=1 << 20,
        )

    block_order = (0, 2, 1, 3) if paired else tuple(range(nb))
    if paired:
        cuts = [0, *(size * c for c in PAIRED_CUTS if size * c < hidden), hidden]
        chunks = list(zip(cuts[:-1], cuts[1:]))
        away = [gate_up((1, 3), *chunk, BF16) for chunk in chunks]
        held, away[0] = lax.optimization_barrier((cot, away[0]))
        far_cot = swap_blk(held, nb, 2)
        features = call(
            functools.partial(features_kernel, halves),
            sds((nb * rows, depth), BF16),
            [piece for p in block_order for piece in x[p]],
            [VMEM] * (nb * halves),
            nbytes=3 << 20,
        )
        kept = [gate_up((0, 2), *chunk, F32) for chunk in chunks]
        near = [swap_blk(a, nb, 1) for a in away]
        pair = [
            call(add_kernel, sds(k.shape, BF16), (k, n), [VMEM] * 2, nbytes=1 << 18)
            for k, n in zip(kept, near)
        ]
        far_cot, pair[1] = lax.optimization_barrier((far_cot, pair[1]))
        far = [swap_blk(p, nb, 2) for p in pair]
        own = [
            call(
                functools.partial(pair_swiglu_kernel, at, size),
                sds((2 * rows, 2 * (to - at)), BF16),
                (kept[c], near[c], far[c], cot, far_cot),
                [VMEM] * 5,
                nbytes=1 << 18,
            )
            for c, (at, to) in enumerate(chunks)
        ]
        parts = [[o, swap_blk(o, nb, 1)] for o in own]
    else:
        chunks = [(0, hidden)]
        features = call(
            functools.partial(features_kernel, halves),
            sds((nb * rows, depth), BF16),
            [piece for p in block_order for piece in x[p]],
            [VMEM] * (nb * halves),
            nbytes=3 << 20,
        )
        partial = [gate_up((p,), 0, hidden, BF16 if p else F32) for p in range(nb)]
        own = call(
            functools.partial(swiglu_kernel, size),
            sds((rows, 2 * hidden), BF16),
            (partial[0], *(swap_blk(partial[p], nb, p) for p in range(1, nb)), cot),
            [VMEM] * (nb + 1),
            nbytes=1 << 20,
        )
        parts = [[own] + [swap_blk(own, nb, p) for p in range(1, nb)]]

    def buffers(at, to):
        return [
            pltpu.VMEM((nb * rows, 2 * (to - at)), BF16),
            pltpu.VMEM(((to - at) // size, 2 * depth, size), F32),
        ]

    finished = []
    for (at, to), part in zip(chunks[:-1], parts):
        finished = [
            call(
                functools.partial(chunk_kernel, at, size, not finished),
                sds((depth, 2, hidden), BF16),
                (*finished, *part, features),
                [VMEM] * (len(finished) + len(part) + 1),
                scratch=buffers(at, to),
                nbytes=1 << 20,
                aliases={0: 0} if finished else {},
            )
        ]
    at, to = chunks[-1]
    step = min(128, depth)
    gradient = call(
        functools.partial(gradient_kernel, at, size),
        sds((depth, 2, hidden), BF16),
        (*finished, *parts[-1], features),
        [VMEM] * (len(finished) + len(parts[-1]) + 1),
        out_specs=HBM,
        scratch=[
            *buffers(at, to),
            pltpu.VMEM((16, 2, 128) if finished else (depth, 2, hidden), BF16),
            pltpu.SemaphoreType.DMA((depth // step,)),
        ],
        nbytes=4 << 20,
    )
    return gradient[:, None]


def solution(mesh):
    return jax.shard_map(
        local,
        mesh=mesh,
        in_specs=(
            P(("group", "blk"), None),
            P(("group", "blk"), None),
            P(("group", "blk"), None, "att"),
            P("blk", "group", None, "att"),
            P("blk", "group", None, "att"),
        ),
        out_specs=P("blk", "group", None, "att"),
        check_vma=False,
    )
```

```python
import functools

import jax
import jax.numpy as jnp
from jax import lax
from jax.experimental import pallas as pl
from jax.experimental.pallas import tpu as pltpu
from jax.sharding import PartitionSpec as P

CAP = 16
BF16 = jnp.bfloat16
F32 = jnp.float32
VMEM_BYTES = 40 * 1024 * 1024


def call(kernel, out_shape, args, in_specs, out_specs=None, scratch=(), flops=0, nbytes=0, aliases=None):
    vmem = pl.BlockSpec(memory_space=pltpu.VMEM)
    return pl.pallas_call(
        kernel,
        out_shape=out_shape,
        in_specs=in_specs,
        out_specs=jax.tree.map(lambda _: vmem, out_shape) if out_specs is None else out_specs,
        scratch_shapes=scratch,
        input_output_aliases=aliases or {},
        compiler_params=pltpu.CompilerParams(vmem_limit_bytes=VMEM_BYTES),
        cost_estimate=pl.CostEstimate(flops=flops, bytes_accessed=nbytes, transcendentals=0),
    )(*args)


VMEM = pl.BlockSpec(memory_space=pltpu.VMEM)
SMEM = pl.BlockSpec(memory_space=pltpu.SMEM)
HBM = pl.BlockSpec(memory_space=pltpu.HBM)


def dot(a, b, dims=((1,), (0,))):
    return lax.dot_general(a, b, (dims, ((), ())), preferred_element_type=F32)


def iota(shape, dim):
    return lax.broadcasted_iota(jnp.int32, shape, dim)


def own_half(halves):
    return lax.axis_index("att") if halves == 2 else 0


def group_partner(ng, k):
    return ng - k if k else 0


def pack_kernel(ng, nb, halves, tokens, routed, act, *refs):
    outs, (token_buf, routed_buf, act_buf, sem) = refs[:ng], refs[ng:]
    top, count = routed.shape
    rows = ng * CAP
    width = tokens.shape[1] // (nb * halves)
    group, block, half = lax.axis_index("group"), lax.axis_index("blk"), own_half(halves)
    copies = [pltpu.make_async_copy(routed, routed_buf, sem.at[0])]
    for p in range(nb):
        partner = block ^ p
        start = pl.multiple_of((partner * halves + half) * width, width)
        copies.append(
            pltpu.make_async_copy(tokens.at[:, pl.ds(start, width)], token_buf.at[p], sem.at[1 + p])
        )
    first = len(copies)
    size = count // 4
    for k in range(4):
        at = pl.ds(k * size, size)
        copies.append(pltpu.make_async_copy(act.at[at], act_buf.at[at], sem.at[first + k]))
    for copy in copies:
        copy.start()
    upto = (iota((count, count), 0) <= iota((count, count), 1)).astype(F32).astype(BF16)
    spread = (iota((count, count * top), 1) // top == iota((count, count * top), 0)).astype(F32).astype(BF16)
    own_slot = iota((top, count * top), 1) % top == iota((top, count * top), 0)
    slot = (iota((rows, count), 0) % CAP + 1).astype(F32)
    slots = iota((rows, 1), 0) // CAP
    expert = (group ^ jnp.where(slots == 0, 0, ng - slots)).astype(F32)
    copies[0].wait()
    ids = routed_buf[...]
    chosen = [jnp.sum((ids == (group ^ group_partner(ng, s))).astype(F32), axis=0, keepdims=True) for s in range(ng)]
    chosen_rows = jnp.concatenate([jnp.broadcast_to(c, (CAP, count)) for c in chosen], axis=0)
    place = dot(chosen_rows.astype(BF16), upto)
    selector = jnp.where(place == slot, chosen_rows, 0.0).astype(BF16)
    ids_wide = dot(ids.astype(F32).astype(BF16), spread)
    ids_flat = jnp.sum(jnp.where(own_slot, ids_wide, 0.0), axis=0, keepdims=True)
    pair = jnp.where(ids_flat == expert, dot(selector, spread), 0.0).astype(BF16)
    for p in range(nb):
        copies[1 + p].wait()
        part = dot(selector, token_buf[p]).astype(BF16)
        for s in range(ng):
            outs[s][:, p * width : (p + 1) * width] = part[s * CAP : (s + 1) * CAP]
    for copy in copies[first:]:
        copy.wait()
    hidden = act.shape[2]
    cot = dot(pair, act_buf[...].reshape(count * top, hidden)).astype(BF16)
    for s in range(ng):
        outs[s][:, nb * width :] = cot[s * CAP : (s + 1) * CAP]


def regroup_kernel(ng, nb, width, *refs):
    pieces, outs = refs[:ng], refs[ng:]
    for s in range(ng):
        at = slice(s * CAP, (s + 1) * CAP)
        for p in range(nb):
            outs[p][at, :] = pieces[s][:, p * width : (p + 1) * width]
        outs[nb][at, :] = pieces[s][:, nb * width :]


def weights_kernel(halves, scales, codes_hbm, out, codes, sem):
    depth, _, hidden = codes.shape
    blocks, _, cols = scales.shape
    qrows, qcols = depth // blocks, hidden // cols
    half = own_half(halves)
    per_half = blocks // halves
    copies = []
    for h in range(halves):
        at = pl.ds(pl.multiple_of((half ^ h) * (depth // halves), depth // halves), depth // halves)
        to = slice(h * (depth // halves), (h + 1) * (depth // halves))
        copies.append(pltpu.make_async_copy(codes_hbm.at[at], codes.at[to], sem.at[h]))
        copies[-1].start()
    pick = [
        (iota((qrows, 2 * qrows), 1) == 2 * iota((qrows, 2 * qrows), 0) + j).astype(F32).astype(BF16)
        for j in range(2)
    ]
    for h in range(halves):
        copies[h].wait()
        for k in range(per_half):
            q, source = h * per_half + k, (half ^ h) * per_half + k
            to = slice(q * qrows, (q + 1) * qrows)
            rows = codes[to].reshape(2 * qrows, hidden)
            for j in range(2):
                values = dot(pick[j], rows)
                for c in range(cols):
                    at = (2 * c + j) * qcols
                    out[to, at : at + qcols] = (
                        values[:, c * qcols : (c + 1) * qcols] * scales[source, j, c]
                    ).astype(BF16)


def gate_up_kernel(halves, at, *refs):
    blocks, weights, out = refs[:-2], refs[-2], refs[-1]
    rows, width = blocks[0].shape[0], weights.shape[0] // halves
    cols = slice(at, at + out.shape[1])
    for i in range(len(blocks) // halves):
        total = dot(blocks[halves * i][:, :width], weights[:width, cols])
        for h in range(1, halves):
            total += dot(blocks[halves * i + h][:, :width], weights[h * width : (h + 1) * width, cols])
        out[i * rows : (i + 1) * rows, :] = total.astype(out.dtype)


def features_kernel(halves, *refs):
    blocks, out = refs[:-1], refs[-1]
    rows, width = blocks[0].shape[0], out.shape[1] // halves
    half = own_half(halves)
    for i in range(len(blocks) // halves):
        for h in range(halves):
            start = pl.multiple_of((half ^ h) * width, width)
            out[i * rows : (i + 1) * rows, pl.ds(start, width)] = blocks[halves * i + h][:, :width]


def add_kernel(kept, arrived, out):
    out[...] = (kept[...] + arrived[...].astype(F32)).astype(BF16)


def swiglu(total, cot, out):
    size = cot.shape[1]
    gate, up = total[:, :size], total[:, size:]
    c = cot.astype(F32)
    s = jax.nn.sigmoid(gate)
    out[:, :size] = (c * up * s * (1.0 + gate * (1.0 - s))).astype(BF16)
    out[:, size:] = (c * gate * s).astype(BF16)


def pair_swiglu_kernel(at, size, kept, near, far, cot, far_cot, out):
    rows = cot.shape[0]
    total = kept[...] + near[...].astype(F32)
    total += jnp.concatenate([far[rows:, :], far[:rows, :]], axis=0).astype(F32)
    for c in range(out.shape[1] // (2 * size)):
        cols = slice(2 * c * size, 2 * (c + 1) * size)
        h = at + c * size
        cots = [cot[:, h : h + size], far_cot[:, h : h + size]]
        swiglu(total[:, cols], jnp.concatenate(cots, axis=0), out.at[:, cols])


def swiglu_kernel(size, *refs):
    parts, cot, out = refs[:-2], refs[-2], refs[-1]
    total = parts[0][...]
    for part in parts[1:]:
        total += part[...].astype(F32)
    for c in range(cot.shape[1] // size):
        cols = slice(2 * c * size, 2 * (c + 1) * size)
        swiglu(total[:, cols], cot[:, c * size : (c + 1) * size], out.at[:, cols])


def gradient_chunk(parts, features, size, stacked, rows, out, written):
    count, depth = parts[0].shape[0], features.shape[1]
    for i, part in enumerate(parts):
        stacked[i * count : (i + 1) * count, :] = part[...]
    step = min(128, depth)
    for k in range(depth // step):
        d = slice(k * step, (k + 1) * step)
        values = dot(features[:, d], stacked[...], ((0,), (0,)))
        for c in range(stacked.shape[1] // (2 * size)):
            for j in range(2):
                at = (2 * c + j) * size
                rows[c, pl.ds(2 * k * step + j, step, stride=2), :] = values[:, at : at + size]
            both = rows[c, 2 * k * step : 2 * (k + 1) * step, :].astype(BF16)
            out[d, :, c * size : (c + 1) * size] = both.reshape(step, 2, size)
        written(k, d)


def chunk_kernel(at, size, first, *refs):
    *parts, features, out, stacked, rows = refs if first else refs[1:]
    out = out.at[:, :, at : at + stacked.shape[1] // 2]
    gradient_chunk(parts, features, size, stacked, rows, out, lambda k, d: None)


def gradient_kernel(at, size, *refs):
    finished, (*parts, features, out, stacked, rows, buf, sem) = refs[: at > 0], refs[at > 0 :]
    whole = finished[0] if finished else buf
    copies = []

    def copy(k, d):
        copies.append(pltpu.make_async_copy(whole.at[d], out.at[d], sem.at[k]))
        copies[-1].start()

    gradient_chunk(parts, features, size, stacked, rows, whole.at[:, :, at:], copy)
    for item in copies:
        item.wait()


def swap_group(x, size, k):
    s = group_partner(size, k)
    return lax.ppermute(x, "group", [(i, i ^ s) for i in range(size)])


def swap_blk(x, size, p):
    return lax.ppermute(x, "blk", [(i, i ^ p) for i in range(size)])


def swap_att(x):
    return lax.ppermute(x, "att", [(0, 1), (1, 0)])


def local(tokens, routed_experts, act_cotangent, weight_codes, weight_scales):
    ng, nb, na = lax.axis_size("group"), lax.axis_size("blk"), lax.axis_size("att")
    depth, _, _, hidden = weight_codes.shape
    halves = 2 if na == 2 and depth % 256 == 0 else 1
    width = depth // halves
    rows = ng * CAP
    sds = jax.ShapeDtypeStruct
    top, count = routed_experts.shape[1], tokens.shape[0]
    sent = call(
        functools.partial(pack_kernel, ng, nb, halves),
        [sds((CAP, nb * width + hidden), BF16)] * ng,
        [pltpu.with_memory_space_constraint(a, pltpu.HBM) for a in (tokens, routed_experts.T, act_cotangent)],
        [HBM, HBM, HBM],
        scratch=[
            pltpu.VMEM((nb, count, width), BF16),
            pltpu.VMEM((top, count), jnp.int32),
            pltpu.VMEM(act_cotangent.shape, BF16),
            pltpu.SemaphoreType.DMA((5 + nb,)),
        ],
        nbytes=2 << 20,
    )
    codes, *sent = lax.optimization_barrier((weight_codes, *sent))
    weights = call(
        functools.partial(weights_kernel, halves),
        sds((depth, 2 * hidden), BF16),
        (weight_scales[:, 0].astype(F32), pltpu.with_memory_space_constraint(codes[:, 0], pltpu.HBM)),
        [SMEM, HBM],
        scratch=[
            pltpu.VMEM((depth, 2, hidden), BF16),
            pltpu.SemaphoreType.DMA((weight_scales.shape[0],)),
        ],
        nbytes=4 << 20,
    )
    pieces = [sent[0]] + [swap_group(sent[s], ng, s) for s in range(1, ng)]
    weights, *pieces = lax.optimization_barrier((weights, *pieces))
    paired = halves == 2 and nb == 4
    *columns, cot = call(
        functools.partial(regroup_kernel, ng, nb, width),
        [sds((rows, width), BF16)] * nb + [sds((rows, hidden), BF16)],
        pieces,
        [VMEM] * ng,
        nbytes=1 << 20,
    )
    size = hidden // weight_scales.shape[3]
    x = {0: [columns[0]]} | {p: [swap_blk(columns[p], nb, p)] for p in range(1, nb)}
    if halves == 2:
        x = {p: [piece, swap_att(piece)] for p, (piece,) in x.items()}

    def gate_up(blocks, at, to, dtype):
        return call(
            functools.partial(gate_up_kernel, halves, 2 * at),
            sds((len(blocks) * rows, 2 * (to - at)), dtype),
            (*(piece for p in blocks for piece in x[p]), weights),
            [VMEM] * (len(blocks) * halves + 1),
            nbytes=1 << 20,
        )

    block_order = (0, 2, 1, 3) if paired else tuple(range(nb))
    if paired:
        chunks = [(at, at + size) for at in range(0, hidden, size)]
        away = [gate_up((1, 3), *chunk, BF16) for chunk in chunks]
        held, away[0] = lax.optimization_barrier((cot, away[0]))
        far_cot = swap_blk(held, nb, 2)
        features = call(
            functools.partial(features_kernel, halves),
            sds((nb * rows, depth), BF16),
            [piece for p in block_order for piece in x[p]],
            [VMEM] * (nb * halves),
            nbytes=3 << 20,
        )
        kept = [gate_up((0, 2), *chunk, F32) for chunk in chunks]
        near = [swap_blk(a, nb, 1) for a in away]
        pair = [
            call(add_kernel, sds(k.shape, BF16), (k, n), [VMEM] * 2, nbytes=1 << 18)
            for k, n in zip(kept, near)
        ]
        far_cot, pair[1 % len(pair)] = lax.optimization_barrier((far_cot, pair[1 % len(pair)]))
        far = [swap_blk(p, nb, 2) for p in pair]
        own = [
            call(
                functools.partial(pair_swiglu_kernel, at, size),
                sds((2 * rows, 2 * (to - at)), BF16),
                (kept[c], near[c], far[c], cot, far_cot),
                [VMEM] * 5,
                nbytes=1 << 18,
            )
            for c, (at, to) in enumerate(chunks)
        ]
        parts = [[o, swap_blk(o, nb, 1)] for o in own]
    else:
        chunks = [(0, hidden)]
        features = call(
            functools.partial(features_kernel, halves),
            sds((nb * rows, depth), BF16),
            [piece for p in block_order for piece in x[p]],
            [VMEM] * (nb * halves),
            nbytes=3 << 20,
        )
        partial = [gate_up((p,), 0, hidden, BF16 if p else F32) for p in range(nb)]
        own = call(
            functools.partial(swiglu_kernel, size),
            sds((rows, 2 * hidden), BF16),
            (partial[0], *(swap_blk(partial[p], nb, p) for p in range(1, nb)), cot),
            [VMEM] * (nb + 1),
            nbytes=1 << 20,
        )
        parts = [[own] + [swap_blk(own, nb, p) for p in range(1, nb)]]

    def buffers(at, to):
        return [
            pltpu.VMEM((nb * rows, 2 * (to - at)), BF16),
            pltpu.VMEM(((to - at) // size, 2 * depth, size), F32),
        ]

    finished = []
    for (at, to), part in zip(chunks[:-1], parts):
        finished = [
            call(
                functools.partial(chunk_kernel, at, size, not finished),
                sds((depth, 2, hidden), BF16),
                (*finished, *part, features),
                [VMEM] * (len(finished) + len(part) + 1),
                scratch=buffers(at, to),
                nbytes=1 << 20,
                aliases={0: 0} if finished else {},
            )
        ]
    at, to = chunks[-1]
    step = min(128, depth)
    gradient = call(
        functools.partial(gradient_kernel, at, size),
        sds((depth, 2, hidden), BF16),
        (*finished, *parts[-1], features),
        [VMEM] * (len(finished) + len(parts[-1]) + 1),
        out_specs=HBM,
        scratch=[
            *buffers(at, to),
            pltpu.VMEM((16, 2, 128) if finished else (depth, 2, hidden), BF16),
            pltpu.SemaphoreType.DMA((depth // step,)),
        ],
        nbytes=4 << 20,
    )
    return gradient[:, None]


def solution(mesh):
    return jax.shard_map(
        local,
        mesh=mesh,
        in_specs=(
            P(("group", "blk"), None),
            P(("group", "blk"), None),
            P(("group", "blk"), None, "att"),
            P("blk", "group", None, "att"),
            P("blk", "group", None, "att"),
        ),
        out_specs=P("blk", "group", None, "att"),
        check_vma=False,
    )
```

```python
import functools

import jax
import jax.numpy as jnp
from jax import lax
from jax.experimental import pallas as pl
from jax.experimental.pallas import tpu as pltpu
from jax.sharding import PartitionSpec as P

CAP = 16
BF16 = jnp.bfloat16
F32 = jnp.float32
VMEM_BYTES = 40 * 1024 * 1024


def call(kernel, out_shape, args, in_specs, out_specs=None, scratch=(), flops=0, nbytes=0, aliases=None):
    vmem = pl.BlockSpec(memory_space=pltpu.VMEM)
    return pl.pallas_call(
        kernel,
        out_shape=out_shape,
        in_specs=in_specs,
        out_specs=jax.tree.map(lambda _: vmem, out_shape) if out_specs is None else out_specs,
        scratch_shapes=scratch,
        input_output_aliases=aliases or {},
        compiler_params=pltpu.CompilerParams(vmem_limit_bytes=VMEM_BYTES),
        cost_estimate=pl.CostEstimate(flops=flops, bytes_accessed=nbytes, transcendentals=0),
    )(*args)


VMEM = pl.BlockSpec(memory_space=pltpu.VMEM)
SMEM = pl.BlockSpec(memory_space=pltpu.SMEM)
HBM = pl.BlockSpec(memory_space=pltpu.HBM)


def dot(a, b, dims=((1,), (0,))):
    return lax.dot_general(a, b, (dims, ((), ())), preferred_element_type=F32)


def iota(shape, dim):
    return lax.broadcasted_iota(jnp.int32, shape, dim)


def own_half(halves):
    return lax.axis_index("att") if halves == 2 else 0


def group_partner(ng, k):
    return ng - k if k else 0


def pack_kernel(ng, nb, halves, tokens, routed, act, *refs):
    outs, (token_buf, routed_buf, act_buf, sem) = refs[:ng], refs[ng:]
    top, count = routed.shape
    rows = ng * CAP
    width = tokens.shape[1] // (nb * halves)
    group, block, half = lax.axis_index("group"), lax.axis_index("blk"), own_half(halves)
    copies = [pltpu.make_async_copy(routed, routed_buf, sem.at[0])]
    for p in range(nb):
        partner = block ^ p
        start = pl.multiple_of((partner * halves + half) * width, width)
        copies.append(
            pltpu.make_async_copy(tokens.at[:, pl.ds(start, width)], token_buf.at[p], sem.at[1 + p])
        )
    first = len(copies)
    size = count // 4
    for k in range(4):
        at = pl.ds(k * size, size)
        copies.append(pltpu.make_async_copy(act.at[at], act_buf.at[at], sem.at[first + k]))
    for copy in copies:
        copy.start()
    upto = (iota((count, count), 0) <= iota((count, count), 1)).astype(F32).astype(BF16)
    spread = (iota((count, count * top), 1) // top == iota((count, count * top), 0)).astype(F32).astype(BF16)
    own_slot = iota((top, count * top), 1) % top == iota((top, count * top), 0)
    slot = (iota((rows, count), 0) % CAP + 1).astype(F32)
    slots = iota((rows, 1), 0) // CAP
    expert = (group ^ jnp.where(slots == 0, 0, ng - slots)).astype(F32)
    copies[0].wait()
    ids = routed_buf[...]
    chosen = [jnp.sum((ids == (group ^ group_partner(ng, s))).astype(F32), axis=0, keepdims=True) for s in range(ng)]
    chosen_rows = jnp.concatenate([jnp.broadcast_to(c, (CAP, count)) for c in chosen], axis=0)
    place = dot(chosen_rows.astype(BF16), upto)
    selector = jnp.where(place == slot, chosen_rows, 0.0).astype(BF16)
    ids_wide = dot(ids.astype(F32).astype(BF16), spread)
    ids_flat = jnp.sum(jnp.where(own_slot, ids_wide, 0.0), axis=0, keepdims=True)
    pair = jnp.where(ids_flat == expert, dot(selector, spread), 0.0).astype(BF16)
    for p in range(nb):
        copies[1 + p].wait()
        part = dot(selector, token_buf[p]).astype(BF16)
        for s in range(ng):
            outs[s][:, p * width : (p + 1) * width] = part[s * CAP : (s + 1) * CAP]
    for copy in copies[first:]:
        copy.wait()
    hidden = act.shape[2]
    cot = dot(pair, act_buf[...].reshape(count * top, hidden)).astype(BF16)
    for s in range(ng):
        outs[s][:, nb * width :] = cot[s * CAP : (s + 1) * CAP]


def regroup_kernel(ng, nb, width, *refs):
    pieces, outs = refs[:ng], refs[ng:]
    for s in range(ng):
        at = slice(s * CAP, (s + 1) * CAP)
        for p in range(nb):
            outs[p][at, :] = pieces[s][:, p * width : (p + 1) * width]
        outs[nb][at, :] = pieces[s][:, nb * width :]


def weights_kernel(halves, scales, codes_hbm, out, codes, sem):
    depth, _, hidden = codes.shape
    blocks, _, cols = scales.shape
    qrows, qcols = depth // blocks, hidden // cols
    half = own_half(halves)
    per_half = blocks // halves
    copies = []
    for h in range(halves):
        at = pl.ds(pl.multiple_of((half ^ h) * (depth // halves), depth // halves), depth // halves)
        to = slice(h * (depth // halves), (h + 1) * (depth // halves))
        copies.append(pltpu.make_async_copy(codes_hbm.at[at], codes.at[to], sem.at[h]))
        copies[-1].start()
    pick = [
        (iota((qrows, 2 * qrows), 1) == 2 * iota((qrows, 2 * qrows), 0) + j).astype(F32).astype(BF16)
        for j in range(2)
    ]
    for h in range(halves):
        copies[h].wait()
        for k in range(per_half):
            q, source = h * per_half + k, (half ^ h) * per_half + k
            to = slice(q * qrows, (q + 1) * qrows)
            rows = codes[to].reshape(2 * qrows, hidden)
            for j in range(2):
                values = dot(pick[j], rows)
                for c in range(cols):
                    at = (2 * c + j) * qcols
                    out[to, at : at + qcols] = (
                        values[:, c * qcols : (c + 1) * qcols] * scales[source, j, c]
                    ).astype(BF16)


def gate_up_kernel(halves, at, *refs):
    blocks, weights, out = refs[:-2], refs[-2], refs[-1]
    rows, width = blocks[0].shape[0], weights.shape[0] // halves
    cols = slice(at, at + out.shape[1])
    for i in range(len(blocks) // halves):
        total = dot(blocks[halves * i][:, :width], weights[:width, cols])
        for h in range(1, halves):
            total += dot(blocks[halves * i + h][:, :width], weights[h * width : (h + 1) * width, cols])
        out[i * rows : (i + 1) * rows, :] = total.astype(out.dtype)


def features_kernel(halves, *refs):
    blocks, out = refs[:-1], refs[-1]
    rows, width = blocks[0].shape[0], out.shape[1] // halves
    half = own_half(halves)
    for i in range(len(blocks) // halves):
        for h in range(halves):
            start = pl.multiple_of((half ^ h) * width, width)
            out[i * rows : (i + 1) * rows, pl.ds(start, width)] = blocks[halves * i + h][:, :width]


def add_kernel(arrived, kept, out):
    out[...] = (kept[...] + arrived[...].astype(F32)).astype(BF16)


def swiglu(total, cot, out):
    size = cot.shape[1]
    gate, up = total[:, :size], total[:, size:]
    c = cot.astype(F32)
    s = jax.nn.sigmoid(gate)
    out[:, :size] = (c * up * s * (1.0 + gate * (1.0 - s))).astype(BF16)
    out[:, size:] = (c * gate * s).astype(BF16)


def pair_swiglu_kernel(at, size, kept, near, far, cot, far_cot, out):
    rows = cot.shape[0]
    total = kept[...] + near[...].astype(F32)
    total += jnp.concatenate([far[rows:, :], far[:rows, :]], axis=0).astype(F32)
    for c in range(out.shape[1] // (2 * size)):
        cols = slice(2 * c * size, 2 * (c + 1) * size)
        h = at + c * size
        cots = [cot[:, h : h + size], far_cot[:, h : h + size]]
        swiglu(total[:, cols], jnp.concatenate(cots, axis=0), out.at[:, cols])


def swiglu_kernel(size, *refs):
    parts, cot, out = refs[:-2], refs[-2], refs[-1]
    total = parts[0][...]
    for part in parts[1:]:
        total += part[...].astype(F32)
    for c in range(cot.shape[1] // size):
        cols = slice(2 * c * size, 2 * (c + 1) * size)
        swiglu(total[:, cols], cot[:, c * size : (c + 1) * size], out.at[:, cols])


def gradient_chunk(parts, features, size, stacked, rows, out, written):
    count, depth = parts[0].shape[0], features.shape[1]
    for i, part in enumerate(parts):
        stacked[i * count : (i + 1) * count, :] = part[...]
    step = min(128, depth)
    for k in range(depth // step):
        d = slice(k * step, (k + 1) * step)
        values = dot(features[:, d], stacked[...], ((0,), (0,)))
        for c in range(stacked.shape[1] // (2 * size)):
            for j in range(2):
                at = (2 * c + j) * size
                rows[c, pl.ds(2 * k * step + j, step, stride=2), :] = values[:, at : at + size]
            both = rows[c, 2 * k * step : 2 * (k + 1) * step, :].astype(BF16)
            out[d, :, c * size : (c + 1) * size] = both.reshape(step, 2, size)
        written(k, d)


def chunk_kernel(at, size, first, *refs):
    *parts, features, out, stacked, rows = refs if first else refs[1:]
    out = out.at[:, :, at : at + stacked.shape[1] // 2]
    gradient_chunk(parts, features, size, stacked, rows, out, lambda k, d: None)


def gradient_kernel(at, size, *refs):
    finished, (*parts, features, out, stacked, rows, buf, sem) = refs[: at > 0], refs[at > 0 :]
    whole = finished[0] if finished else buf
    copies = []

    def copy(k, d):
        copies.append(pltpu.make_async_copy(whole.at[d], out.at[d], sem.at[k]))
        copies[-1].start()

    gradient_chunk(parts, features, size, stacked, rows, whole.at[:, :, at:], copy)
    for item in copies:
        item.wait()


def swap_group(x, size, k):
    s = group_partner(size, k)
    return lax.ppermute(x, "group", [(i, i ^ s) for i in range(size)])


def swap_blk(x, size, p):
    return lax.ppermute(x, "blk", [(i, i ^ p) for i in range(size)])


def swap_att(x):
    return lax.ppermute(x, "att", [(0, 1), (1, 0)])


def local(tokens, routed_experts, act_cotangent, weight_codes, weight_scales):
    ng, nb, na = lax.axis_size("group"), lax.axis_size("blk"), lax.axis_size("att")
    depth, _, _, hidden = weight_codes.shape
    halves = 2 if na == 2 and depth % 256 == 0 else 1
    width = depth // halves
    rows = ng * CAP
    sds = jax.ShapeDtypeStruct
    top, count = routed_experts.shape[1], tokens.shape[0]
    sent = call(
        functools.partial(pack_kernel, ng, nb, halves),
        [sds((CAP, nb * width + hidden), BF16)] * ng,
        [pltpu.with_memory_space_constraint(a, pltpu.HBM) for a in (tokens, routed_experts.T, act_cotangent)],
        [HBM, HBM, HBM],
        scratch=[
            pltpu.VMEM((nb, count, width), BF16),
            pltpu.VMEM((top, count), jnp.int32),
            pltpu.VMEM(act_cotangent.shape, BF16),
            pltpu.SemaphoreType.DMA((5 + nb,)),
        ],
        nbytes=2 << 20,
    )
    codes, *sent = lax.optimization_barrier((weight_codes, *sent))
    weights = call(
        functools.partial(weights_kernel, halves),
        sds((depth, 2 * hidden), BF16),
        (weight_scales[:, 0].astype(F32), pltpu.with_memory_space_constraint(codes[:, 0], pltpu.HBM)),
        [SMEM, HBM],
        scratch=[
            pltpu.VMEM((depth, 2, hidden), BF16),
            pltpu.SemaphoreType.DMA((weight_scales.shape[0],)),
        ],
        nbytes=4 << 20,
    )
    pieces = [sent[0]] + [swap_group(sent[s], ng, s) for s in range(1, ng)]
    weights, *pieces = lax.optimization_barrier((weights, *pieces))
    paired = halves == 2 and nb == 4
    *columns, cot = call(
        functools.partial(regroup_kernel, ng, nb, width),
        [sds((rows, width), BF16)] * nb + [sds((rows, hidden), BF16)],
        pieces,
        [VMEM] * ng,
        nbytes=1 << 20,
    )
    size = hidden // weight_scales.shape[3]
    x = {0: [columns[0]]} | {p: [swap_blk(columns[p], nb, p)] for p in range(1, nb)}
    if halves == 2:
        x = {p: [piece, swap_att(piece)] for p, (piece,) in x.items()}

    def gate_up(blocks, at, to, dtype):
        return call(
            functools.partial(gate_up_kernel, halves, 2 * at),
            sds((len(blocks) * rows, 2 * (to - at)), dtype),
            (*(piece for p in blocks for piece in x[p]), weights),
            [VMEM] * (len(blocks) * halves + 1),
            nbytes=1 << 20,
        )

    block_order = (0, 2, 1, 3) if paired else tuple(range(nb))
    if paired:
        chunks = [(at, at + size) for at in range(0, hidden, size)]
        away = [gate_up((1, 3), *chunk, BF16) for chunk in chunks]
        held, away[0] = lax.optimization_barrier((cot, away[0]))
        far_cot = swap_blk(held, nb, 2)
        features = call(
            functools.partial(features_kernel, halves),
            sds((nb * rows, depth), BF16),
            [piece for p in block_order for piece in x[p]],
            [VMEM] * (nb * halves),
            nbytes=3 << 20,
        )
        kept = [gate_up((0, 2), *chunk, F32) for chunk in chunks]
        near = [swap_blk(a, nb, 1) for a in away]
        pair = [
            call(add_kernel, sds(k.shape, BF16), (n, k), [VMEM] * 2, nbytes=1 << 18)
            for k, n in zip(kept, near)
        ]
        far_cot, pair[1 % len(pair)] = lax.optimization_barrier((far_cot, pair[1 % len(pair)]))
        far = [swap_blk(p, nb, 2) for p in pair]
        own = [
            call(
                functools.partial(pair_swiglu_kernel, at, size),
                sds((2 * rows, 2 * (to - at)), BF16),
                (kept[c], near[c], far[c], cot, far_cot),
                [VMEM] * 5,
                nbytes=1 << 18,
            )
            for c, (at, to) in enumerate(chunks)
        ]
        parts = [[o, swap_blk(o, nb, 1)] for o in own]
    else:
        chunks = [(0, hidden)]
        features = call(
            functools.partial(features_kernel, halves),
            sds((nb * rows, depth), BF16),
            [piece for p in block_order for piece in x[p]],
            [VMEM] * (nb * halves),
            nbytes=3 << 20,
        )
        partial = [gate_up((p,), 0, hidden, BF16 if p else F32) for p in range(nb)]
        own = call(
            functools.partial(swiglu_kernel, size),
            sds((rows, 2 * hidden), BF16),
            (partial[0], *(swap_blk(partial[p], nb, p) for p in range(1, nb)), cot),
            [VMEM] * (nb + 1),
            nbytes=1 << 20,
        )
        parts = [[own] + [swap_blk(own, nb, p) for p in range(1, nb)]]

    def buffers(at, to):
        return [
            pltpu.VMEM((nb * rows, 2 * (to - at)), BF16),
            pltpu.VMEM(((to - at) // size, 2 * depth + 8, size), F32),
        ]

    finished = []
    for (at, to), part in zip(chunks[:-1], parts):
        finished = [
            call(
                functools.partial(chunk_kernel, at, size, not finished),
                sds((depth, 2, hidden), BF16),
                (*finished, *part, features),
                [VMEM] * (len(finished) + len(part) + 1),
                scratch=buffers(at, to),
                nbytes=1 << 20,
                aliases={0: 0} if finished else {},
            )
        ]
    at, to = chunks[-1]
    step = min(128, depth)
    gradient = call(
        functools.partial(gradient_kernel, at, size),
        sds((depth, 2, hidden), BF16),
        (*finished, *parts[-1], features),
        [VMEM] * (len(finished) + len(parts[-1]) + 1),
        out_specs=HBM,
        scratch=[
            *buffers(at, to),
            pltpu.VMEM((16, 2, 128) if finished else (depth, 2, hidden), BF16),
            pltpu.SemaphoreType.DMA((depth // step,)),
        ],
        nbytes=4 << 20,
    )
    return gradient[:, None]


def solution(mesh):
    return jax.shard_map(
        local,
        mesh=mesh,
        in_specs=(
            P(("group", "blk"), None),
            P(("group", "blk"), None),
            P(("group", "blk"), None, "att"),
            P("blk", "group", None, "att"),
            P("blk", "group", None, "att"),
        ),
        out_specs=P("blk", "group", None, "att"),
        check_vma=False,
    )
```

```python
import functools

import jax
import jax.numpy as jnp
from jax import lax
from jax.experimental import pallas as pl
from jax.experimental.pallas import tpu as pltpu
from jax.sharding import PartitionSpec as P

CAP = 16
BF16 = jnp.bfloat16
F32 = jnp.float32
VMEM_BYTES = 40 * 1024 * 1024


def call(kernel, out_shape, args, in_specs, out_specs=None, scratch=(), flops=0, nbytes=0, aliases=None):
    vmem = pl.BlockSpec(memory_space=pltpu.VMEM)
    return pl.pallas_call(
        kernel,
        out_shape=out_shape,
        in_specs=in_specs,
        out_specs=jax.tree.map(lambda _: vmem, out_shape) if out_specs is None else out_specs,
        scratch_shapes=scratch,
        input_output_aliases=aliases or {},
        compiler_params=pltpu.CompilerParams(vmem_limit_bytes=VMEM_BYTES),
        cost_estimate=pl.CostEstimate(flops=flops, bytes_accessed=nbytes, transcendentals=0),
    )(*args)


VMEM = pl.BlockSpec(memory_space=pltpu.VMEM)
SMEM = pl.BlockSpec(memory_space=pltpu.SMEM)
HBM = pl.BlockSpec(memory_space=pltpu.HBM)


def dot(a, b, dims=((1,), (0,))):
    return lax.dot_general(a, b, (dims, ((), ())), preferred_element_type=F32)


def iota(shape, dim):
    return lax.broadcasted_iota(jnp.int32, shape, dim)


def own_half(halves):
    return lax.axis_index("att") if halves == 2 else 0


def group_partner(ng, k):
    return ng - k if k else 0


def pack_kernel(ng, nb, halves, tokens, routed, act, *refs):
    outs, (token_buf, routed_buf, act_buf, sem) = refs[:ng], refs[ng:]
    top, count = routed.shape
    rows = ng * CAP
    width = tokens.shape[1] // (nb * halves)
    group, block, half = lax.axis_index("group"), lax.axis_index("blk"), own_half(halves)
    copies = [pltpu.make_async_copy(routed, routed_buf, sem.at[0])]
    for p in range(nb):
        partner = block ^ p
        start = pl.multiple_of((partner * halves + half) * width, width)
        copies.append(
            pltpu.make_async_copy(tokens.at[:, pl.ds(start, width)], token_buf.at[p], sem.at[1 + p])
        )
    first = len(copies)
    size = count // 4
    for k in range(4):
        at = pl.ds(k * size, size)
        copies.append(pltpu.make_async_copy(act.at[at], act_buf.at[at], sem.at[first + k]))
    for copy in copies:
        copy.start()
    upto = (iota((count, count), 0) <= iota((count, count), 1)).astype(F32).astype(BF16)
    spread = (iota((count, count * top), 1) // top == iota((count, count * top), 0)).astype(F32).astype(BF16)
    own_slot = iota((top, count * top), 1) % top == iota((top, count * top), 0)
    slot = (iota((rows, count), 0) % CAP + 1).astype(F32)
    slots = iota((rows, 1), 0) // CAP
    expert = (group ^ jnp.where(slots == 0, 0, ng - slots)).astype(F32)
    copies[0].wait()
    ids = routed_buf[...]
    chosen = [jnp.sum((ids == (group ^ group_partner(ng, s))).astype(F32), axis=0, keepdims=True) for s in range(ng)]
    chosen_rows = jnp.concatenate([jnp.broadcast_to(c, (CAP, count)) for c in chosen], axis=0)
    place = dot(chosen_rows.astype(BF16), upto)
    selector = jnp.where(place == slot, chosen_rows, 0.0).astype(BF16)
    ids_wide = dot(ids.astype(F32).astype(BF16), spread)
    ids_flat = jnp.sum(jnp.where(own_slot, ids_wide, 0.0), axis=0, keepdims=True)
    pair = jnp.where(ids_flat == expert, dot(selector, spread), 0.0).astype(BF16)
    for p in range(nb):
        copies[1 + p].wait()
        part = dot(selector, token_buf[p]).astype(BF16)
        for s in range(ng):
            outs[s][:, p * width : (p + 1) * width] = part[s * CAP : (s + 1) * CAP]
    for copy in copies[first:]:
        copy.wait()
    hidden = act.shape[2]
    cot = dot(pair, act_buf[...].reshape(count * top, hidden)).astype(BF16)
    for s in range(ng):
        outs[s][:, nb * width :] = cot[s * CAP : (s + 1) * CAP]


def regroup_kernel(ng, nb, width, *refs):
    pieces, outs = refs[:ng], refs[ng:]
    for s in range(ng):
        at = slice(s * CAP, (s + 1) * CAP)
        for p in range(nb):
            outs[p][at, :] = pieces[s][:, p * width : (p + 1) * width]
        outs[nb][at, :] = pieces[s][:, nb * width :]


def weights_kernel(halves, scales, codes_hbm, out, codes, sem):
    depth, _, hidden = codes.shape
    blocks, _, cols = scales.shape
    qrows, qcols = depth // blocks, hidden // cols
    half = own_half(halves)
    per_half = blocks // halves
    copies = []
    for h in range(halves):
        at = pl.ds(pl.multiple_of((half ^ h) * (depth // halves), depth // halves), depth // halves)
        to = slice(h * (depth // halves), (h + 1) * (depth // halves))
        copies.append(pltpu.make_async_copy(codes_hbm.at[at], codes.at[to], sem.at[h]))
        copies[-1].start()
    pick = [
        (iota((qrows, 2 * qrows), 1) == 2 * iota((qrows, 2 * qrows), 0) + j).astype(F32).astype(BF16)
        for j in range(2)
    ]
    for h in range(halves):
        copies[h].wait()
        for k in range(per_half):
            q, source = h * per_half + k, (half ^ h) * per_half + k
            to = slice(q * qrows, (q + 1) * qrows)
            rows = codes[to].reshape(2 * qrows, hidden)
            for j in range(2):
                values = dot(pick[j], rows)
                for c in range(cols):
                    at = (2 * c + j) * qcols
                    out[to, at : at + qcols] = (
                        values[:, c * qcols : (c + 1) * qcols] * scales[source, j, c]
                    ).astype(BF16)


def gate_up_kernel(halves, at, *refs):
    blocks, weights, out = refs[:-2], refs[-2], refs[-1]
    rows, width = blocks[0].shape[0], weights.shape[0] // halves
    cols = slice(at, at + out.shape[1])
    for i in range(len(blocks) // halves):
        total = dot(blocks[halves * i][:, :width], weights[:width, cols])
        for h in range(1, halves):
            total += dot(blocks[halves * i + h][:, :width], weights[h * width : (h + 1) * width, cols])
        out[i * rows : (i + 1) * rows, :] = total.astype(out.dtype)


def features_kernel(halves, *refs):
    blocks, out = refs[:-1], refs[-1]
    rows, width = blocks[0].shape[0], out.shape[0] // halves
    half = own_half(halves)
    for h in range(halves):
        start = pl.multiple_of((half ^ h) * width, width)
        side = [blocks[halves * i + h][:, :width] for i in range(len(blocks) // halves)]
        out[pl.ds(start, width), :] = jnp.concatenate(side, axis=0).T


def add_kernel(arrived, kept, out):
    out[...] = (kept[...] + arrived[...].astype(F32)).astype(BF16)


def swiglu(total, cot, out):
    size = cot.shape[1]
    gate, up = total[:, :size], total[:, size:]
    c = cot.astype(F32)
    s = jax.nn.sigmoid(gate)
    out[:, :size] = (c * up * s * (1.0 + gate * (1.0 - s))).astype(BF16)
    out[:, size:] = (c * gate * s).astype(BF16)


def pair_swiglu_kernel(at, size, kept, near, far, cot, far_cot, out):
    rows = cot.shape[0]
    total = kept[...] + near[...].astype(F32)
    total += jnp.concatenate([far[rows:, :], far[:rows, :]], axis=0).astype(F32)
    for c in range(out.shape[1] // (2 * size)):
        cols = slice(2 * c * size, 2 * (c + 1) * size)
        h = at + c * size
        cots = [cot[:, h : h + size], far_cot[:, h : h + size]]
        swiglu(total[:, cols], jnp.concatenate(cots, axis=0), out.at[:, cols])


def swiglu_kernel(size, *refs):
    parts, cot, out = refs[:-2], refs[-2], refs[-1]
    total = parts[0][...]
    for part in parts[1:]:
        total += part[...].astype(F32)
    for c in range(cot.shape[1] // size):
        cols = slice(2 * c * size, 2 * (c + 1) * size)
        swiglu(total[:, cols], cot[:, c * size : (c + 1) * size], out.at[:, cols])


def gradient_chunk(parts, features, size, stacked, rows, out, written):
    count, depth = parts[0].shape[0], features.shape[0]
    for i, part in enumerate(parts):
        stacked[i * count : (i + 1) * count, :] = part[...]
    step = min(128, depth)
    for k in range(depth // step):
        d = slice(k * step, (k + 1) * step)
        values = dot(features[d, :], stacked[...])
        for c in range(stacked.shape[1] // (2 * size)):
            for j in range(2):
                at = (2 * c + j) * size
                rows[c, pl.ds(2 * k * step + j, step, stride=2), :] = values[:, at : at + size]
            both = rows[c, 2 * k * step : 2 * (k + 1) * step, :].astype(BF16)
            out[d, :, c * size : (c + 1) * size] = both.reshape(step, 2, size)
        written(k, d)


def chunk_kernel(at, size, first, *refs):
    *parts, features, out, stacked, rows = refs if first else refs[1:]
    out = out.at[:, :, at : at + stacked.shape[1] // 2]
    gradient_chunk(parts, features, size, stacked, rows, out, lambda k, d: None)


def gradient_kernel(at, size, *refs):
    finished, (*parts, features, out, stacked, rows, buf, sem) = refs[: at > 0], refs[at > 0 :]
    whole = finished[0] if finished else buf
    copies = []

    def copy(k, d):
        copies.append(pltpu.make_async_copy(whole.at[d], out.at[d], sem.at[k]))
        copies[-1].start()

    gradient_chunk(parts, features, size, stacked, rows, whole.at[:, :, at:], copy)
    for item in copies:
        item.wait()


def swap_group(x, size, k):
    s = group_partner(size, k)
    return lax.ppermute(x, "group", [(i, i ^ s) for i in range(size)])


def swap_blk(x, size, p):
    return lax.ppermute(x, "blk", [(i, i ^ p) for i in range(size)])


def swap_att(x):
    return lax.ppermute(x, "att", [(0, 1), (1, 0)])


def local(tokens, routed_experts, act_cotangent, weight_codes, weight_scales):
    ng, nb, na = lax.axis_size("group"), lax.axis_size("blk"), lax.axis_size("att")
    depth, _, _, hidden = weight_codes.shape
    halves = 2 if na == 2 and depth % 256 == 0 else 1
    width = depth // halves
    rows = ng * CAP
    sds = jax.ShapeDtypeStruct
    top, count = routed_experts.shape[1], tokens.shape[0]
    sent = call(
        functools.partial(pack_kernel, ng, nb, halves),
        [sds((CAP, nb * width + hidden), BF16)] * ng,
        [pltpu.with_memory_space_constraint(a, pltpu.HBM) for a in (tokens, routed_experts.T, act_cotangent)],
        [HBM, HBM, HBM],
        scratch=[
            pltpu.VMEM((nb, count, width), BF16),
            pltpu.VMEM((top, count), jnp.int32),
            pltpu.VMEM(act_cotangent.shape, BF16),
            pltpu.SemaphoreType.DMA((5 + nb,)),
        ],
        nbytes=2 << 20,
    )
    codes, *sent = lax.optimization_barrier((weight_codes, *sent))
    weights = call(
        functools.partial(weights_kernel, halves),
        sds((depth, 2 * hidden), BF16),
        (weight_scales[:, 0].astype(F32), pltpu.with_memory_space_constraint(codes[:, 0], pltpu.HBM)),
        [SMEM, HBM],
        scratch=[
            pltpu.VMEM((depth, 2, hidden), BF16),
            pltpu.SemaphoreType.DMA((weight_scales.shape[0],)),
        ],
        nbytes=4 << 20,
    )
    pieces = [sent[0]] + [swap_group(sent[s], ng, s) for s in range(1, ng)]
    weights, *pieces = lax.optimization_barrier((weights, *pieces))
    paired = halves == 2 and nb == 4
    *columns, cot = call(
        functools.partial(regroup_kernel, ng, nb, width),
        [sds((rows, width), BF16)] * nb + [sds((rows, hidden), BF16)],
        pieces,
        [VMEM] * ng,
        nbytes=1 << 20,
    )
    size = hidden // weight_scales.shape[3]
    x = {0: [columns[0]]} | {p: [swap_blk(columns[p], nb, p)] for p in range(1, nb)}
    if halves == 2:
        x = {p: [piece, swap_att(piece)] for p, (piece,) in x.items()}

    def gate_up(blocks, at, to, dtype):
        return call(
            functools.partial(gate_up_kernel, halves, 2 * at),
            sds((len(blocks) * rows, 2 * (to - at)), dtype),
            (*(piece for p in blocks for piece in x[p]), weights),
            [VMEM] * (len(blocks) * halves + 1),
            nbytes=1 << 20,
        )

    block_order = (0, 2, 1, 3) if paired else tuple(range(nb))
    if paired:
        chunks = [(at, at + size) for at in range(0, hidden, size)]
        away = [gate_up((1, 3), *chunk, BF16) for chunk in chunks]
        held, away[0] = lax.optimization_barrier((cot, away[0]))
        far_cot = swap_blk(held, nb, 2)
        features = call(
            functools.partial(features_kernel, halves),
            sds((depth, nb * rows), BF16),
            [piece for p in block_order for piece in x[p]],
            [VMEM] * (nb * halves),
            nbytes=3 << 20,
        )
        kept = [gate_up((0, 2), *chunk, F32) for chunk in chunks]
        near = [swap_blk(a, nb, 1) for a in away]
        pair = [
            call(add_kernel, sds(k.shape, BF16), (n, k), [VMEM] * 2, nbytes=1 << 18)
            for k, n in zip(kept, near)
        ]
        far_cot, pair[1 % len(pair)] = lax.optimization_barrier((far_cot, pair[1 % len(pair)]))
        far = [swap_blk(p, nb, 2) for p in pair]
        own = [
            call(
                functools.partial(pair_swiglu_kernel, at, size),
                sds((2 * rows, 2 * (to - at)), BF16),
                (kept[c], near[c], far[c], cot, far_cot),
                [VMEM] * 5,
                nbytes=1 << 18,
            )
            for c, (at, to) in enumerate(chunks)
        ]
        parts = [[o, swap_blk(o, nb, 1)] for o in own]
    else:
        chunks = [(0, hidden)]
        features = call(
            functools.partial(features_kernel, halves),
            sds((depth, nb * rows), BF16),
            [piece for p in block_order for piece in x[p]],
            [VMEM] * (nb * halves),
            nbytes=3 << 20,
        )
        partial = [gate_up((p,), 0, hidden, BF16 if p else F32) for p in range(nb)]
        own = call(
            functools.partial(swiglu_kernel, size),
            sds((rows, 2 * hidden), BF16),
            (partial[0], *(swap_blk(partial[p], nb, p) for p in range(1, nb)), cot),
            [VMEM] * (nb + 1),
            nbytes=1 << 20,
        )
        parts = [[own] + [swap_blk(own, nb, p) for p in range(1, nb)]]

    def buffers(at, to):
        return [
            pltpu.VMEM((nb * rows, 2 * (to - at)), BF16),
            pltpu.VMEM(((to - at) // size, 2 * depth + 8, size), F32),
        ]

    finished = []
    for (at, to), part in zip(chunks[:-1], parts):
        finished = [
            call(
                functools.partial(chunk_kernel, at, size, not finished),
                sds((depth, 2, hidden), BF16),
                (*finished, *part, features),
                [VMEM] * (len(finished) + len(part) + 1),
                scratch=buffers(at, to),
                nbytes=1 << 20,
                aliases={0: 0} if finished else {},
            )
        ]
    at, to = chunks[-1]
    step = min(128, depth)
    gradient = call(
        functools.partial(gradient_kernel, at, size),
        sds((depth, 2, hidden), BF16),
        (*finished, *parts[-1], features),
        [VMEM] * (len(finished) + len(parts[-1]) + 1),
        out_specs=HBM,
        scratch=[
            *buffers(at, to),
            pltpu.VMEM((16, 2, 128) if finished else (depth, 2, hidden), BF16),
            pltpu.SemaphoreType.DMA((depth // step,)),
        ],
        nbytes=4 << 20,
    )
    return gradient[:, None]


def solution(mesh):
    return jax.shard_map(
        local,
        mesh=mesh,
        in_specs=(
            P(("group", "blk"), None),
            P(("group", "blk"), None),
            P(("group", "blk"), None, "att"),
            P("blk", "group", None, "att"),
            P("blk", "group", None, "att"),
        ),
        out_specs=P("blk", "group", None, "att"),
        check_vma=False,
    )
```
